32 devices in a mesh: seq: 4 (over y, x), segment: 8 (over z, core).
Axes of the slice: x: 2, y: 2, z: 4, core: 2. Of those that a mesh axis runs over, the one named last changes fastest.
Arguments:
- stream: bfloat16 [512, 32768], P('seq', 'segment'), may hold values from -6 to 6
- w_query: bfloat16 [4096, 16384], P(None, 'segment'), may hold values from -0.09375 to 0.09375
- w_out: bfloat16 [16384, 4096], P('segment'), may hold values from -0.125 to 0.125
- neighbour_kv: bfloat16 [2, 2, 2048, 16384], P(None, None, 'seq', 'segment'), may hold values from -6 to 6
Outputs:
- first: bfloat16 [512, 32768], P('seq', 'segment')
- second: bfloat16 [512, 32768], P('seq', 'segment')
The draws below stay inside these ranges and needn't reach their ends.
All inputs are finite; a program needn't handle non-finite values.
Results may differ from the reference program's by a relative error of at most 0.0075.
Values may be sent and summed in bfloat16 or wider, within the bound.
A program may use at most 128 MiB of HBM per device.

```python
import jax
import jax.numpy as jnp
from jax import lax

D = 4096
HD = 128
HEADS = 16
SECT = 8
CH = 64
NEIGH = 2
NBL = 128
TICKS = 2
HG = 1
TOKENS = 512
NBTOK = 2048


def steps_of(key, shape, cuts, low, largest):
    level = 1.0
    for position, parts in cuts:
        draws = jax.random.uniform(jax.random.fold_in(jax.random.fold_in(key, 6), position), (parts,), jnp.float32, low / len(cuts), largest / len(cuts))
        level = level * jnp.repeat(jnp.exp(draws), shape[position] // parts).reshape((-1,) + (1,) * (len(shape) - 1 - position))
    return level


def noise(stream_key, shape, width, bound, split=(), dtype=jnp.bfloat16):
    factor_of = steps_of(stream_key, shape, split, -0.22, 0.18) if split else 1.0
    values = jax.random.normal(stream_key, shape, jnp.float32) * width * factor_of
    return jnp.minimum(jnp.maximum(values, -bound), bound).astype(dtype)


def setup_inputs(seed: int = 0) -> dict:
    arg_keys = jax.random.split(jax.random.key(seed), 5)
    stream = noise(arg_keys[0], (TOKENS, SECT * D), 1.0, 6.0, ((0, 4), (1, 8)))
    w_query = noise(arg_keys[1], (D, SECT * HEADS * HD), D ** -0.5, 0.09375, ((1, 8),))
    w_out = noise(arg_keys[2], (SECT * HEADS * HD, D), (HEADS * HD) ** -0.5, 0.125, ((0, 8),))
    neighbour_kv = noise(arg_keys[3], (TICKS, 2, NBTOK, SECT * HEADS * HD), 1.0, 6.0, ((2, 4), (3, 8)))
    return dict(stream=stream, w_query=w_query, w_out=w_out, neighbour_kv=neighbour_kv)


EPS = 1e-05

def cross_layer(rows_in, keys_values, weight_query, weight_out):
    wide = rows_in.astype(jnp.float32)
    normed = (wide * lax.rsqrt(lax.optimization_barrier(jnp.mean(wide * wide, axis=-1, keepdims=True)) + EPS)).astype(jnp.bfloat16)
    queries = jnp.dot(normed, weight_query, preferred_element_type=jnp.float32).astype(jnp.bfloat16)
    tokens = queries.shape[0]
    spans = tokens // CH
    head_cols = HEADS * HD
    padded = jnp.concatenate([jnp.zeros((1, head_cols), jnp.bfloat16), queries, jnp.zeros((CH - 1, head_cols), jnp.bfloat16)], axis=0)
    grouped = padded.reshape(spans + 1, CH, HEADS, HD)[1:]
    keys = keys_values[0].reshape(spans, NEIGH * NBL, HEADS, HD)
    values = keys_values[1].reshape(spans, NEIGH * NBL, HEADS, HD)
    scores = jnp.einsum('gchd,gkhd->ghck', grouped.astype(jnp.float32), keys.astype(jnp.float32)) * HD ** (-0.5)
    exponent = jnp.exp(scores)
    weights = (exponent / lax.optimization_barrier(jnp.sum(exponent, axis=-1, keepdims=True))).astype(jnp.bfloat16)
    attended = jnp.einsum('ghck,gkhd->gchd', weights.astype(jnp.float32), values.astype(jnp.float32)).astype(jnp.bfloat16)
    attended = jnp.concatenate([jnp.zeros((1, CH, HEADS, HD), jnp.bfloat16), attended], axis=0)
    attended = attended.reshape(-1, head_cols)[1:1 + tokens]
    group_cols = head_cols // HG
    total = wide
    for group_no in range(HG):
        term = jnp.dot(attended[:, group_no * group_cols:(group_no + 1) * group_cols], weight_out[group_no * group_cols:(group_no + 1) * group_cols, :], preferred_element_type=jnp.float32).astype(jnp.bfloat16)
        term = lax.optimization_barrier(term)
        total = total + term.astype(jnp.float32)
    return total.astype(jnp.bfloat16)

def reference(stream, w_query, w_out, neighbour_kv):
    head_cols = HEADS * HD
    firsts = []
    for section in range(SECT):
        firsts.append(cross_layer(stream[:, section * D:(section + 1) * D], neighbour_kv[0][:, :, section * head_cols:(section + 1) * head_cols], w_query[:, section * head_cols:(section + 1) * head_cols], w_out[section * head_cols:(section + 1) * head_cols, :]))
    seconds = []
    for section in range(SECT):
        if section > 0:
            inputs = firsts[section - 1]
        else:
            inputs = jnp.zeros_like(firsts[0])
        seconds.append(cross_layer(inputs, neighbour_kv[1][:, :, section * head_cols:(section + 1) * head_cols], w_query[:, section * head_cols:(section + 1) * head_cols], w_out[section * head_cols:(section + 1) * head_cols, :]))
    return (jnp.concatenate(firsts, axis=1), jnp.concatenate(seconds, axis=1))
```

```python
import jax
import jax.numpy as jnp
from jax import lax
from jax.experimental import pallas as pl
from jax.experimental.pallas import tpu as pltpu
from jax.sharding import PartitionSpec as P

HD = 128
SECT = 8
CH = 64
NEIGH = 2
NBL = 128
TICKS = 2


EPS = 1e-05


def swapped(block, axis, apart):
    count = lax.axis_size(axis)
    route = []
    for low in range(count):
        high = low | 1 << apart
        if high != low and high < count:
            route += [(low, high), (high, low)]
    return lax.ppermute(block, axis, route)


def passed_along(block, axis, distance):
    devices = range(lax.axis_size(axis))
    route = [(i - distance, i) for i in devices if i - distance in devices]
    return lax.ppermute(block, axis, route)


def assemble(piece, head_group, bit_order, total_bits):
    current = piece
    for bit_index in bit_order:
        other = swapped(current, "segment", bit_index)
        is_upper = head_group // 2**bit_index % 2 == 1
        lower_half = jnp.where(is_upper, other, current)
        upper_half = jnp.where(is_upper, current, other)
        current = jnp.stack([lower_half, upper_half], axis=1)
    count_bits = len(bit_order)
    permutation = [0]
    for target in range(count_bits):
        wanted = total_bits - 1 - target
        permutation.append(1 + (count_bits - 1 - bit_order.index(wanted)))
    permutation.append(count_bits + 1)
    if count_bits > 0:
        current = jnp.transpose(current, permutation)
    return current.reshape(piece.shape[0], -1)


def share_sums(term, head_group, bit_order, total_bits):
    partial_value = term.astype(jnp.float32)
    tok_rows = partial_value.shape[0]
    current = partial_value.reshape(
        (tok_rows,) + (2,) * total_bits + (partial_value.shape[1] // 2**total_bits,)
    )
    remaining = list(range(total_bits - 1, -1, -1))
    for bit_index in bit_order:
        axis_pos = 1 + remaining.index(bit_index)
        lower_half = lax.index_in_dim(current, 0, axis_pos, keepdims=False)
        upper_half = lax.index_in_dim(current, 1, axis_pos, keepdims=False)
        is_upper = head_group // 2**bit_index % 2 == 1
        kept_half = jnp.where(is_upper, upper_half, lower_half)
        sent_half = jnp.where(is_upper, lower_half, upper_half)
        current = kept_half + swapped(sent_half.astype(jnp.bfloat16), "segment", bit_index).astype(
            sent_half.dtype
        )
        remaining = [bit_left for bit_left in remaining if bit_left != bit_index]
    return current


def local_layer(whole, keys_values, edge_kv, w_query, w_out):
    wide = whole.astype(jnp.float32)
    normed = (wide * lax.rsqrt(jnp.mean(wide * wide, axis=-1, keepdims=True) + EPS)).astype(
        jnp.bfloat16
    )
    queries = jnp.dot(normed, w_query, preferred_element_type=jnp.float32).astype(jnp.bfloat16)
    tokens = queries.shape[0]
    head_cols = queries.shape[1]
    groups = tokens // CH + 1
    padded = jnp.concatenate(
        [
            jnp.zeros((1, head_cols), jnp.bfloat16),
            queries,
            jnp.zeros((CH - 1, head_cols), jnp.bfloat16),
        ],
        axis=0,
    )
    padded = padded.reshape(groups, CH, head_cols // HD, HD)
    extended = jnp.concatenate([edge_kv, keys_values], axis=1).reshape(
        2, groups, NEIGH * NBL, head_cols // HD, HD
    )
    scores = jnp.einsum(
        "gchd,gkhd->ghck", padded, extended[0], preferred_element_type=jnp.float32
    ) * HD ** (-0.5)
    exponent = jnp.exp(scores)
    weights = (exponent / jnp.sum(exponent, axis=-1, keepdims=True)).astype(jnp.bfloat16)
    attended = jnp.einsum(
        "ghck,gkhd->gchd", weights, extended[1], preferred_element_type=jnp.float32
    ).astype(jnp.bfloat16)
    attended = attended.reshape(-1, head_cols)[1 : 1 + tokens]
    term = jnp.dot(attended, w_out, preferred_element_type=jnp.float32).astype(jnp.bfloat16)
    return lax.optimization_barrier(term)


MESH = pl.DeviceIdType.MESH
LAG = 2
AHEAD = 4


def relay_kernel(
    x_hbm, wq_hbm, wo_hbm, kv_hbm, first_hbm, second_hbm,
    x_v, wq_v, wo_v, kv_v, x2_v, y_v, y2_v, acc_v, q_v, hq_v, ha_v, hr_v, att_v, r_v,
    x_sem, wq_sem, wo_sem, kv_sem, hq_send, hq_recv, ha_send, ha_recv,
    rel_send, rel_recv, out_sem,
):
    nq, width, cw = wq_v.shape
    nf, cols, fw = wo_v.shape
    keys = kv_v.shape[3]
    half = keys // 2
    k, s = lax.axis_index("seq"), lax.axis_index("segment")
    nk, ns = lax.axis_size("seq"), lax.axis_size("segment")
    has_prev, has_next = k > 0, k < nk - 1
    has_in, has_out = s > 0, s < ns - 1
    prev = (lax.rem(k + nk - 1, nk), s)
    following = (lax.rem(k + 1, nk), s)
    below = (k, lax.rem(s + ns - 1, ns))
    above = (k, lax.rem(s + 1, ns))
    top, low = pl.ds(0, CH), pl.ds(CH, CH)
    last_row = lax.broadcasted_iota(jnp.int32, (CH, cw), 0) == CH - 1

    def head_cols(n):
        return pl.ds(pl.multiple_of(n * cw, cw), cw)

    def feature_cols(c):
        return pl.ds(pl.multiple_of(c * fw, fw), fw)

    def load_wq(c):
        return pltpu.make_async_copy(wq_hbm.at[:, head_cols(c)], wq_v.at[c], wq_sem.at[c])

    def load_kv(t, c):
        return pltpu.make_async_copy(
            kv_hbm.at[t, :, :, head_cols(c)], kv_v.at[t, c], kv_sem.at[t, c]
        )

    def load_wo(c):
        return pltpu.make_async_copy(wo_hbm.at[:, feature_cols(c)], wo_v.at[c], wo_sem.at[c])

    def halo_q(t, n):
        return pltpu.make_async_remote_copy(
            src_ref=q_v.at[t, n, top], dst_ref=hq_v.at[t, n],
            send_sem=hq_send.at[t, n], recv_sem=hq_recv.at[t, n],
            device_id=prev, device_id_type=MESH,
        )

    def halo_a(t, n):
        return pltpu.make_async_remote_copy(
            src_ref=ha_v.at[t, n], dst_ref=hr_v.at[t, n],
            send_sem=ha_send.at[t, n], recv_sem=ha_recv.at[t, n],
            device_id=following, device_id_type=MESH,
        )

    def relay(b, c):
        rows = pl.ds(b * CH, CH)
        return pltpu.make_async_remote_copy(
            src_ref=y_v.at[c, rows], dst_ref=x2_v.at[c, rows],
            send_sem=rel_send.at[b, c], recv_sem=rel_recv.at[b, c],
            device_id=above, device_id_type=MESH,
        )

    def store(t, c):
        buffer, target = ((y_v, first_hbm), (y2_v, second_hbm))[t]
        return pltpu.make_async_copy(
            buffer.at[c], target.at[:, feature_cols(c)], out_sem.at[t, c]
        )

    def attend(block, t, n, own_first):
        row = lax.broadcasted_iota(jnp.int32, (CH, keys), 0)
        key = lax.broadcasted_iota(jnp.int32, (CH, keys), 1)
        valid = jnp.logical_xor(row == CH - 1, (key < half) if own_first else (key >= half))
        parts = []
        for h in range(cw // HD):
            at = slice(h * HD, (h + 1) * HD)
            scores = lax.dot_general(
                block[:, at], kv_v[t, n, 0, :, at], (((1,), (1,)), ((), ())),
                preferred_element_type=jnp.float32,
            )
            scores = jnp.where(valid, scores, -3e38)
            most = jnp.max(scores, axis=1, keepdims=True)
            exponent = jnp.exp((scores - most) * HD ** (-0.5))
            share = 1.0 / jnp.sum(exponent, axis=1, keepdims=True)
            weights = (exponent * share).astype(jnp.bfloat16)
            parts.append(
                jnp.dot(weights, kv_v[t, n, 1, :, at], preferred_element_type=jnp.float32)
            )
        return jnp.concatenate(parts, axis=1).astype(jnp.bfloat16)

    def own_block(t, n):
        att_v[low, head_cols(n)] = attend(q_v[t, n, low], t, n, True)

    def halo_block(t, n):
        @pl.when(has_next)
        def _():
            halo_q(t, n).wait_recv()

        block = jnp.where(last_row, q_v[t, n, top], hq_v[t, n])
        ha_v[t, n] = attend(block, t, n, False)

        @pl.when(has_next)
        def _():
            halo_a(t, n).start()

    def returned(t, n):
        @pl.when(has_prev)
        def _():
            halo_a(t, n).wait_recv()

        att_v[top, head_cols(n)] = jnp.where(last_row, ha_v[t, n], hr_v[t, n])

    def loop(start, stop, body):
        def step(i, carry):
            body(i)
            return carry

        lax.fori_loop(start, stop, step, 0)

    load_x = pltpu.make_async_copy(x_hbm, x_v, x_sem)
    load_x.start()
    for c in range(AHEAD):
        load_wq(c).start()
        load_kv(0, c).start()

    barrier = pltpu.get_barrier_semaphore()
    pairs = ((has_prev, prev), (has_next, following), (has_in, below), (has_out, above))
    for exists, device in pairs:

        @pl.when(exists)
        def _(device=device):
            pl.semaphore_signal(barrier, inc=1, device_id=device, device_id_type=MESH)

    @pl.when(jnp.logical_not(has_next))
    def _():
        hq_v[...] = jnp.zeros_like(hq_v)

    @pl.when(jnp.logical_not(has_prev))
    def _():
        hr_v[...] = jnp.zeros_like(hr_v)

    @pl.when(jnp.logical_not(has_in))
    def _():
        x2_v[...] = jnp.zeros_like(x2_v)

    acc_v[...] = jnp.zeros_like(acc_v)
    load_x.wait()
    wide = x_v[...].astype(jnp.float32)
    scale = lax.rsqrt(jnp.mean(wide * wide, axis=1, keepdims=True) + EPS)
    r_v[...] = jnp.broadcast_to(scale, r_v.shape)
    pl.semaphore_wait(barrier, sum(exists.astype(jnp.int32) for exists, _ in pairs))

    def produce(c):
        load_wq(c).wait()

        @pl.when(c + AHEAD < nq)
        def _():
            load_wq(c + AHEAD).start()
            load_kv(0, c + AHEAD).start()

        @pl.when(c + AHEAD >= nq)
        def _():
            load_wo(c + AHEAD - nq).start()

        total = jnp.dot(x_v[...], wq_v[c], preferred_element_type=jnp.float32)
        q_v[0, c] = (total * r_v[:, :1]).astype(jnp.bfloat16)

        @pl.when(has_prev)
        def _():
            halo_q(0, c).start()

        load_kv(0, c).wait()
        own_block(0, c)

    def produce_and_halo(c):
        produce(c)
        halo_block(0, c - LAG)

    loop(0, LAG, produce)
    loop(LAG, nq, produce_and_halo)
    for c in range(AHEAD, nf):
        load_wo(c).start()
    loop(nq - LAG, nq, lambda n: halo_block(0, n))
    loop(0, nq, lambda n: returned(0, n))

    def project(c):
        term = jnp.dot(att_v[...], wo_v[c], preferred_element_type=jnp.float32)
        return term.astype(jnp.bfloat16).astype(jnp.float32)

    def first_chunk(c):
        load_wo(c).wait()
        load_kv(1, c).start()
        y_v[c] = (x_v[:, feature_cols(c)].astype(jnp.float32) + project(c)).astype(jnp.bfloat16)

        @pl.when(has_out)
        def _():
            relay(0, c).start()

        store(0, c).start()

    loop(0, nf, first_chunk)

    @pl.when(has_out)
    def _():
        loop(0, nf, lambda c: relay(1, c).start())

    def gather(b, c):
        @pl.when(has_in)
        def _():
            relay(b, c).wait_recv()

        rows = pl.ds(b * CH, CH)
        block = x2_v[c, rows]
        for n in range(nq):
            acc_v[n, rows] += jnp.dot(
                block, wq_v[n, feature_cols(c), :], preferred_element_type=jnp.float32
            )

    def row_scale(b):
        rows = pl.ds(b * CH, CH)
        squares = jnp.zeros((CH, 1), jnp.float32)
        for c in range(nf):
            block = x2_v[c, rows].astype(jnp.float32)
            squares += jnp.sum(block * block, axis=1, keepdims=True)
        r_v[rows] = jnp.broadcast_to(lax.rsqrt(squares / width + EPS), (CH, r_v.shape[1]))

    def queries(b, n):
        rows = pl.ds(b * CH, CH)
        q_v[1, n, rows] = (acc_v[n, rows] * r_v[rows, :1]).astype(jnp.bfloat16)

    loop(0, nf, lambda c: gather(0, c))
    row_scale(0)

    def send_queries(n):
        queries(0, n)

        @pl.when(has_prev)
        def _():
            halo_q(1, n).start()

        load_kv(1, n).wait()

    loop(0, nq, send_queries)

    def gather_and_halo(c):
        gather(1, c)
        halo_block(1, c - LAG)

    loop(0, LAG, lambda c: gather(1, c))
    loop(LAG, nq, gather_and_halo)
    loop(nq - LAG, nq, lambda n: halo_block(1, n))
    row_scale(1)

    def finish(n):
        queries(1, n)
        own_block(1, n)

    loop(0, nq, finish)
    loop(0, nq, lambda n: returned(1, n))

    def second_chunk(c):
        y2_v[c] = (x2_v[c].astype(jnp.float32) + project(c)).astype(jnp.bfloat16)
        store(1, c).start()

    loop(0, nf, second_chunk)

    @pl.when(has_prev)
    def _():
        for t in range(TICKS):
            loop(0, nq, lambda n: halo_q(t, n).wait_send())

    @pl.when(has_next)
    def _():
        for t in range(TICKS):
            loop(0, nq, lambda n: halo_a(t, n).wait_send())

    @pl.when(has_out)
    def _():
        for b in range(2):
            loop(0, nf, lambda c: relay(b, c).wait_send())

    for t in range(TICKS):
        loop(0, nf, lambda c: store(t, c).wait())


def relay_call(stream, w_query, w_out, neighbour_kv):
    rows, width = stream.shape
    cols = w_query.shape[1]
    keys = neighbour_kv.shape[2]
    cw = 2 * HD
    nq = cols // cw
    fw = width // nq
    bf16, dma = jnp.bfloat16, pltpu.SemaphoreType.DMA
    hbm = pl.BlockSpec(memory_space=pl.ANY)
    flops = TICKS * 2 * rows * cols * (2 * width + 4 * keys)
    read = 2 * (stream.size + w_query.size + w_out.size + neighbour_kv.size + 2 * stream.size)
    return pl.pallas_call(
        relay_kernel,
        out_shape=[jax.ShapeDtypeStruct(stream.shape, bf16)] * 2,
        in_specs=[hbm] * 4,
        out_specs=[hbm] * 2,
        scratch_shapes=[
            pltpu.VMEM((rows, width), bf16),
            pltpu.VMEM((nq, width, cw), bf16),
            pltpu.VMEM((nq, cols, fw), bf16),
            pltpu.VMEM((TICKS, nq, 2, keys, cw), bf16),
            pltpu.VMEM((nq, rows, fw), bf16),
            pltpu.VMEM((nq, rows, fw), bf16),
            pltpu.VMEM((nq, rows, fw), bf16),
            pltpu.VMEM((nq, rows, cw), jnp.float32),
            pltpu.VMEM((TICKS, nq, rows, cw), bf16),
            pltpu.VMEM((TICKS, nq, CH, cw), bf16),
            pltpu.VMEM((TICKS, nq, CH, cw), bf16),
            pltpu.VMEM((TICKS, nq, CH, cw), bf16),
            pltpu.VMEM((rows, cols), bf16),
            pltpu.VMEM((rows, 128), jnp.float32),
            dma,
            dma((nq,)),
            dma((nq,)),
            dma((TICKS, nq)),
            dma((TICKS, nq)),
            dma((TICKS, nq)),
            dma((TICKS, nq)),
            dma((TICKS, nq)),
            dma((2, nq)),
            dma((2, nq)),
            dma((TICKS, nq)),
        ],
        compiler_params=pltpu.CompilerParams(
            collective_id=0, has_side_effects=True, vmem_limit_bytes=60 * 2**20
        ),
        cost_estimate=pl.CostEstimate(flops=flops, bytes_accessed=read, transcendentals=0),
    )(stream, w_query, w_out, neighbour_kv)


def fits(stream, w_query, neighbour_kv):
    rows, width = stream.shape
    cols = w_query.shape[1]
    return (
        lax.axis_size("segment") == SECT
        and rows == 2 * CH
        and neighbour_kv.shape[2] == 2 * NEIGH * NBL
        and cols % (2 * HD) == 0
        and width % (cols // (2 * HD) * 128) == 0
        and cols // (2 * HD) >= AHEAD
        and 2 * width * cols * 2 + neighbour_kv.size * 2 <= 42 * 2**20
    )


def per_device(stream, w_query, w_out, neighbour_kv):
    if fits(stream, w_query, neighbour_kv):
        return tuple(relay_call(stream, w_query, w_out, neighbour_kv))
    groups_per = lax.axis_size("segment") // SECT
    head_group = lax.axis_index("segment") % groups_per
    total_bits = groups_per.bit_length() - 1
    bit_order = list(range(total_bits))
    edge_rows = NEIGH * NBL
    edges = passed_along(neighbour_kv[:, :, neighbour_kv.shape[2] - edge_rows :, :], "seq", 1)
    current = stream
    whole = assemble(current, head_group, bit_order, total_bits)
    outputs = []
    for tick_no in range(TICKS):
        term = local_layer(whole, neighbour_kv[tick_no], edges[tick_no], w_query, w_out)
        summed = share_sums(term, head_group, bit_order, total_bits)
        result = (current.astype(jnp.float32) + summed).astype(jnp.bfloat16)
        outputs.append(result)
        if tick_no + 1 < TICKS:
            current = passed_along(result, "segment", groups_per)
            whole = assemble(current, head_group, bit_order, total_bits)
    return (outputs[0], outputs[TICKS - 1])


def solution(mesh):
    placed = (
        P("seq", "segment"),
        P(None, "segment"),
        P("segment", None),
        P(None, None, "seq", "segment"),
    )
    return jax.shard_map(
        per_device,
        mesh=mesh,
        in_specs=placed,
        out_specs=(P("seq", "segment"), P("seq", "segment")),
        check_vma=False,
    )
```

```python
import jax
import jax.numpy as jnp
from jax import lax
from jax.experimental import pallas as pl
from jax.experimental.pallas import tpu as pltpu
from jax.sharding import PartitionSpec as P

HD = 128
SECT = 8
CH = 64
NEIGH = 2
NBL = 128
TICKS = 2


EPS = 1e-05


def swapped(block, axis, apart):
    count = lax.axis_size(axis)
    route = []
    for low in range(count):
        high = low | 1 << apart
        if high != low and high < count:
            route += [(low, high), (high, low)]
    return lax.ppermute(block, axis, route)


def passed_along(block, axis, distance):
    devices = range(lax.axis_size(axis))
    route = [(i - distance, i) for i in devices if i - distance in devices]
    return lax.ppermute(block, axis, route)


def assemble(piece, head_group, bit_order, total_bits):
    current = piece
    for bit_index in bit_order:
        other = swapped(current, "segment", bit_index)
        is_upper = head_group // 2**bit_index % 2 == 1
        lower_half = jnp.where(is_upper, other, current)
        upper_half = jnp.where(is_upper, current, other)
        current = jnp.stack([lower_half, upper_half], axis=1)
    count_bits = len(bit_order)
    permutation = [0]
    for target in range(count_bits):
        wanted = total_bits - 1 - target
        permutation.append(1 + (count_bits - 1 - bit_order.index(wanted)))
    permutation.append(count_bits + 1)
    if count_bits > 0:
        current = jnp.transpose(current, permutation)
    return current.reshape(piece.shape[0], -1)


def share_sums(term, head_group, bit_order, total_bits):
    partial_value = term.astype(jnp.float32)
    tok_rows = partial_value.shape[0]
    current = partial_value.reshape(
        (tok_rows,) + (2,) * total_bits + (partial_value.shape[1] // 2**total_bits,)
    )
    remaining = list(range(total_bits - 1, -1, -1))
    for bit_index in bit_order:
        axis_pos = 1 + remaining.index(bit_index)
        lower_half = lax.index_in_dim(current, 0, axis_pos, keepdims=False)
        upper_half = lax.index_in_dim(current, 1, axis_pos, keepdims=False)
        is_upper = head_group // 2**bit_index % 2 == 1
        kept_half = jnp.where(is_upper, upper_half, lower_half)
        sent_half = jnp.where(is_upper, lower_half, upper_half)
        current = kept_half + swapped(sent_half.astype(jnp.bfloat16), "segment", bit_index).astype(
            sent_half.dtype
        )
        remaining = [bit_left for bit_left in remaining if bit_left != bit_index]
    return current


def local_layer(whole, keys_values, edge_kv, w_query, w_out):
    wide = whole.astype(jnp.float32)
    normed = (wide * lax.rsqrt(jnp.mean(wide * wide, axis=-1, keepdims=True) + EPS)).astype(
        jnp.bfloat16
    )
    queries = jnp.dot(normed, w_query, preferred_element_type=jnp.float32).astype(jnp.bfloat16)
    tokens = queries.shape[0]
    head_cols = queries.shape[1]
    groups = tokens // CH + 1
    padded = jnp.concatenate(
        [
            jnp.zeros((1, head_cols), jnp.bfloat16),
            queries,
            jnp.zeros((CH - 1, head_cols), jnp.bfloat16),
        ],
        axis=0,
    )
    padded = padded.reshape(groups, CH, head_cols // HD, HD)
    extended = jnp.concatenate([edge_kv, keys_values], axis=1).reshape(
        2, groups, NEIGH * NBL, head_cols // HD, HD
    )
    scores = jnp.einsum(
        "gchd,gkhd->ghck", padded, extended[0], preferred_element_type=jnp.float32
    ) * HD ** (-0.5)
    exponent = jnp.exp(scores)
    weights = (exponent / jnp.sum(exponent, axis=-1, keepdims=True)).astype(jnp.bfloat16)
    attended = jnp.einsum(
        "ghck,gkhd->gchd", weights, extended[1], preferred_element_type=jnp.float32
    ).astype(jnp.bfloat16)
    attended = attended.reshape(-1, head_cols)[1 : 1 + tokens]
    term = jnp.dot(attended, w_out, preferred_element_type=jnp.float32).astype(jnp.bfloat16)
    return lax.optimization_barrier(term)


MESH = pl.DeviceIdType.MESH
LAG = 3
AHEAD = 4


def relay_kernel(
    x_hbm, wq_hbm, wo_hbm, kv_hbm, first_hbm, second_hbm,
    x_v, wq_v, wo_v, kv_v, x2_v, y_v, y2_v, acc_v, q_v, hq_v, ha_v, hr_v, la_v, att_v, r_v,
    x_sem, wq_sem, wo_sem, kv_sem, hq_send, hq_recv, ha_send, ha_recv,
    rel_send, rel_recv, out_sem,
):
    nq, width, cw = wq_v.shape
    nf, cols, fw = wo_v.shape
    keys = kv_v.shape[3]
    half = keys // 2
    k, s = lax.axis_index("seq"), lax.axis_index("segment")
    nk, ns = lax.axis_size("seq"), lax.axis_size("segment")
    has_prev, has_next = k > 0, k < nk - 1
    has_in, has_out = s > 0, s < ns - 1
    prev = (lax.rem(k + nk - 1, nk), s)
    following = (lax.rem(k + 1, nk), s)
    below = (k, lax.rem(s + ns - 1, ns))
    above = (k, lax.rem(s + 1, ns))
    top, low = pl.ds(0, CH), pl.ds(CH, CH)
    last_row = lax.broadcasted_iota(jnp.int32, (CH, cw), 0) == CH - 1

    def head_cols(n):
        return pl.ds(pl.multiple_of(n * cw, cw), cw)

    def feature_cols(c):
        return pl.ds(pl.multiple_of(c * fw, fw), fw)

    def load_wq(c):
        return pltpu.make_async_copy(wq_hbm.at[:, head_cols(c)], wq_v.at[c], wq_sem.at[c])

    def load_kv(t, c):
        return pltpu.make_async_copy(
            kv_hbm.at[t, :, :, head_cols(c)], kv_v.at[t, c], kv_sem.at[t, c]
        )

    def load_wo(c):
        return pltpu.make_async_copy(wo_hbm.at[:, feature_cols(c)], wo_v.at[c], wo_sem.at[c])

    def halo_q(t, n):
        return pltpu.make_async_remote_copy(
            src_ref=q_v.at[t, n, top], dst_ref=hq_v.at[t, n],
            send_sem=hq_send.at[t, n], recv_sem=hq_recv.at[t, n],
            device_id=prev, device_id_type=MESH,
        )

    def halo_a(t, n):
        return pltpu.make_async_remote_copy(
            src_ref=ha_v.at[t, n], dst_ref=hr_v.at[t, n],
            send_sem=ha_send.at[t, n], recv_sem=ha_recv.at[t, n],
            device_id=following, device_id_type=MESH,
        )

    def relay(b, c):
        rows = pl.ds(b * CH, CH)
        return pltpu.make_async_remote_copy(
            src_ref=y_v.at[c, rows], dst_ref=x2_v.at[c, rows],
            send_sem=rel_send.at[b, c], recv_sem=rel_recv.at[b, c],
            device_id=above, device_id_type=MESH,
        )

    def store(t, c):
        buffer, target = ((y_v, first_hbm), (y2_v, second_hbm))[t]
        return pltpu.make_async_copy(
            buffer.at[c], target.at[:, feature_cols(c)], out_sem.at[t, c]
        )

    ones = jnp.ones((half, HD), jnp.bfloat16)

    def attend(block, t, n, span):
        at_keys = pl.ds(span * half, half)
        parts = []
        for h in range(cw // HD):
            at = slice(h * HD, (h + 1) * HD)
            scores = lax.dot_general(
                block[:, at], kv_v[t, n, 0, at_keys, at], (((1,), (1,)), ((), ())),
                preferred_element_type=jnp.float32,
            )
            most = jnp.max(scores, axis=1, keepdims=True)
            exponent = jnp.exp((scores - most) * HD ** (-0.5)).astype(jnp.bfloat16)
            values = jnp.concatenate([kv_v[t, n, 1, at_keys, at], ones], axis=1)
            both = jnp.dot(exponent, values, preferred_element_type=jnp.float32)
            parts.append(both[:, :HD] / both[:, HD:])
        return jnp.concatenate(parts, axis=1).astype(jnp.bfloat16)

    def loop(start, stop, body):
        def step(i, carry):
            body(i)
            return carry

        lax.fori_loop(start, stop, step, 0)

    load_x = pltpu.make_async_copy(x_hbm, x_v, x_sem)
    load_x.start()
    for c in range(AHEAD):
        load_wq(c).start()
        load_kv(0, c).start()

    barrier = pltpu.get_barrier_semaphore()
    pairs = ((has_prev, prev), (has_next, following), (has_in, below), (has_out, above))
    for exists, device in pairs:

        @pl.when(exists)
        def _(device=device):
            pl.semaphore_signal(barrier, inc=1, device_id=device, device_id_type=MESH)

    @pl.when(jnp.logical_not(has_next))
    def _():
        hq_v[...] = jnp.zeros_like(hq_v)

    @pl.when(jnp.logical_not(has_prev))
    def _():
        hr_v[...] = jnp.zeros_like(hr_v)

    @pl.when(jnp.logical_not(has_in))
    def _():
        x2_v[...] = jnp.zeros_like(x2_v)

    acc_v[...] = jnp.zeros_like(acc_v)
    load_x.wait()
    wide = x_v[...].astype(jnp.float32)
    scale = lax.rsqrt(jnp.mean(wide * wide, axis=1, keepdims=True) + EPS)
    r_v[...] = jnp.broadcast_to(scale, r_v.shape)
    pl.semaphore_wait(barrier, sum(exists.astype(jnp.int32) for exists, _ in pairs))

    def step(c, with_q, with_own, with_halo):
        own, other = c - 1, c - LAG
        if with_q:
            load_wq(c).wait()

            @pl.when(c + AHEAD < nq)
            def _():
                load_wq(c + AHEAD).start()
                load_kv(0, c + AHEAD).start()

            @pl.when(c + AHEAD >= nq)
            def _():
                load_wo(c + AHEAD - nq).start()

        if with_own:
            load_kv(0, own).wait()
        if with_halo:

            @pl.when(has_next)
            def _():
                halo_q(0, other).wait_recv()

        if with_own:
            own_block = jnp.where(last_row, q_v[0, own, top], q_v[0, own, low])
        if with_halo:
            halo_block = jnp.where(last_row, q_v[0, other, low], hq_v[0, other])
        if with_q:
            total = jnp.dot(x_v[...], wq_v[c], preferred_element_type=jnp.float32)
            made = (total * r_v[:, :1]).astype(jnp.bfloat16)
        if with_own:
            own_out = attend(own_block, 0, own, 0)
        if with_halo:
            halo_out = attend(halo_block, 0, other, 1)
        if with_q:
            q_v[0, c] = made
        if with_own:
            la_v[own] = own_out
        if with_halo:
            ha_v[0, other] = halo_out
        if with_q:

            @pl.when(has_prev)
            def _():
                halo_q(0, c).start()

        if with_halo:

            @pl.when(has_next)
            def _():
                halo_a(0, other).start()

    step(0, True, False, False)
    loop(1, LAG, lambda c: step(c, True, True, False))
    loop(LAG, nq, lambda c: step(c, True, True, True))
    for c in range(AHEAD, nf):
        load_wo(c).start()
    step(nq, False, True, True)
    loop(nq + 1, nq + LAG, lambda c: step(c, False, False, True))

    def join(n):
        @pl.when(has_prev)
        def _():
            halo_a(0, n).wait_recv()

        att_v[top, head_cols(n)] = jnp.where(last_row, la_v[n], hr_v[0, n])
        att_v[low, head_cols(n)] = jnp.where(last_row, ha_v[0, n], la_v[n])

    loop(0, nq, join)

    def project(c):
        term = jnp.dot(att_v[...], wo_v[c], preferred_element_type=jnp.float32)
        return term.astype(jnp.bfloat16).astype(jnp.float32)

    def first_chunk(c):
        load_wo(c).wait()
        load_kv(1, c).start()
        y_v[c] = (x_v[:, feature_cols(c)].astype(jnp.float32) + project(c)).astype(jnp.bfloat16)

        @pl.when(has_out)
        def _():
            relay(0, c).start()

        store(0, c).start()

    loop(0, nf, first_chunk)

    @pl.when(has_out)
    def _():
        loop(0, nf, lambda c: relay(1, c).start())

    def wait_rows(b, c):
        @pl.when(has_in)
        def _():
            relay(b, c).wait_recv()

    def gather(b, c):
        rows = pl.ds(b * CH, CH)
        block = x2_v[c, rows]
        for n in range(nq):
            acc_v[n, rows] += jnp.dot(
                block, wq_v[n, feature_cols(c), :], preferred_element_type=jnp.float32
            )

    def gather_first(c):
        wait_rows(0, c)
        gather(0, c)

    def row_scale(b):
        rows = pl.ds(b * CH, CH)
        squares = jnp.zeros((CH, 1), jnp.float32)
        for c in range(nf):
            block = x2_v[c, rows].astype(jnp.float32)
            squares += jnp.sum(block * block, axis=1, keepdims=True)
        r_v[rows] = jnp.broadcast_to(lax.rsqrt(squares / width + EPS), (CH, r_v.shape[1]))

    loop(0, nf, gather_first)
    row_scale(0)
    for n in range(nq):
        q_v[1, n, top] = (acc_v[n, top] * r_v[top, :1]).astype(jnp.bfloat16)

    @pl.when(has_prev)
    def _():
        loop(0, nq, lambda n: halo_q(1, n).start())

    loop(0, nq, lambda n: load_kv(1, n).wait())

    def gather_second(c, with_rows, with_halo):
        other = c - LAG
        if with_rows:
            wait_rows(1, c)
        if with_halo:

            @pl.when(has_next)
            def _():
                halo_q(1, other).wait_recv()

        if with_halo:
            halo_out = attend(hq_v[1, other], 1, other, 1)
        if with_rows:
            gather(1, c)
        if with_halo:
            ha_v[1, other] = halo_out

            @pl.when(has_next)
            def _():
                halo_a(1, other).start()

    loop(0, LAG, lambda c: gather_second(c, True, False))
    loop(LAG, nq, lambda c: gather_second(c, True, True))
    loop(nq, nq + LAG, lambda c: gather_second(c, False, True))
    row_scale(1)
    last_of_tail = lax.broadcasted_iota(jnp.int32, (16, cw), 0) == 15

    def finish(pair):
        results = []
        for n in (2 * pair, 2 * pair + 1):
            mine = (acc_v[n, low] * r_v[low, :1]).astype(jnp.bfloat16)
            out = attend(jnp.where(last_row, q_v[1, n, top], mine), 1, n, 0)
            end = attend(mine[CH - 16:], 1, n, 1)
            end = jnp.where(last_of_tail, end, out[CH - 16:])
            results.append((n, out, jnp.concatenate([out[:CH - 16], end], axis=0)))
        for n, out, rows in results:
            la_v[n] = out
            att_v[low, head_cols(n)] = rows

    loop(0, nq // 2, finish)

    def join_top(n):
        @pl.when(has_prev)
        def _():
            halo_a(1, n).wait_recv()

        att_v[top, head_cols(n)] = jnp.where(last_row, la_v[n], hr_v[1, n])

    loop(0, nq, join_top)

    def second_chunk(c):
        y2_v[c] = (x2_v[c].astype(jnp.float32) + project(c)).astype(jnp.bfloat16)
        store(1, c).start()

    loop(0, nf, second_chunk)

    @pl.when(has_prev)
    def _():
        for t in range(TICKS):
            loop(0, nq, lambda n: halo_q(t, n).wait_send())

    @pl.when(has_next)
    def _():
        for t in range(TICKS):
            loop(0, nq, lambda n: halo_a(t, n).wait_send())

    @pl.when(has_out)
    def _():
        for b in range(2):
            loop(0, nf, lambda c: relay(b, c).wait_send())

    for t in range(TICKS):
        loop(0, nf, lambda c: store(t, c).wait())


def relay_call(stream, w_query, w_out, neighbour_kv):
    rows, width = stream.shape
    cols = w_query.shape[1]
    keys = neighbour_kv.shape[2]
    cw = 2 * HD
    nq = cols // cw
    fw = width // nq
    bf16, dma = jnp.bfloat16, pltpu.SemaphoreType.DMA
    hbm = pl.BlockSpec(memory_space=pl.ANY)
    flops = TICKS * 2 * rows * cols * (2 * width + 4 * keys)
    read = 2 * (stream.size + w_query.size + w_out.size + neighbour_kv.size + 2 * stream.size)
    return pl.pallas_call(
        relay_kernel,
        out_shape=[jax.ShapeDtypeStruct(stream.shape, bf16)] * 2,
        in_specs=[hbm] * 4,
        out_specs=[hbm] * 2,
        scratch_shapes=[
            pltpu.VMEM((rows, width), bf16),
            pltpu.VMEM((nq, width, cw), bf16),
            pltpu.VMEM((nq, cols, fw), bf16),
            pltpu.VMEM((TICKS, nq, 2, keys, cw), bf16),
            pltpu.VMEM((nq, rows, fw), bf16),
            pltpu.VMEM((nq, rows, fw), bf16),
            pltpu.VMEM((nq, rows, fw), bf16),
            pltpu.VMEM((nq, rows, cw), jnp.float32),
            pltpu.VMEM((TICKS, nq, rows, cw), bf16),
            pltpu.VMEM((TICKS, nq, CH, cw), bf16),
            pltpu.VMEM((TICKS, nq, CH, cw), bf16),
            pltpu.VMEM((TICKS, nq, CH, cw), bf16),
            pltpu.VMEM((nq, CH, cw), bf16),
            pltpu.VMEM((rows, cols), bf16),
            pltpu.VMEM((rows, 128), jnp.float32),
            dma,
            dma((nq,)),
            dma((nq,)),
            dma((TICKS, nq)),
            dma((TICKS, nq)),
            dma((TICKS, nq)),
            dma((TICKS, nq)),
            dma((TICKS, nq)),
            dma((2, nq)),
            dma((2, nq)),
            dma((TICKS, nq)),
        ],
        compiler_params=pltpu.CompilerParams(
            collective_id=0, has_side_effects=True, vmem_limit_bytes=60 * 2**20
        ),
        cost_estimate=pl.CostEstimate(flops=flops, bytes_accessed=read, transcendentals=0),
    )(stream, w_query, w_out, neighbour_kv)


def fits(stream, w_query, neighbour_kv):
    rows, width = stream.shape
    cols = w_query.shape[1]
    return (
        lax.axis_size("segment") == SECT
        and rows == 2 * CH
        and neighbour_kv.shape[2] == 2 * NEIGH * NBL
        and cols % (4 * HD) == 0
        and width % (cols // (2 * HD) * 128) == 0
        and cols // (2 * HD) >= AHEAD
        and 2 * width * cols * 2 + neighbour_kv.size * 2 <= 42 * 2**20
    )


def per_device(stream, w_query, w_out, neighbour_kv):
    if fits(stream, w_query, neighbour_kv):
        return tuple(relay_call(stream, w_query, w_out, neighbour_kv))
    groups_per = lax.axis_size("segment") // SECT
    head_group = lax.axis_index("segment") % groups_per
    total_bits = groups_per.bit_length() - 1
    bit_order = list(range(total_bits))
    edge_rows = NEIGH * NBL
    edges = passed_along(neighbour_kv[:, :, neighbour_kv.shape[2] - edge_rows :, :], "seq", 1)
    current = stream
    whole = assemble(current, head_group, bit_order, total_bits)
    outputs = []
    for tick_no in range(TICKS):
        term = local_layer(whole, neighbour_kv[tick_no], edges[tick_no], w_query, w_out)
        summed = share_sums(term, head_group, bit_order, total_bits)
        result = (current.astype(jnp.float32) + summed).astype(jnp.bfloat16)
        outputs.append(result)
        if tick_no + 1 < TICKS:
            current = passed_along(result, "segment", groups_per)
            whole = assemble(current, head_group, bit_order, total_bits)
    return (outputs[0], outputs[TICKS - 1])


def solution(mesh):
    placed = (
        P("seq", "segment"),
        P(None, "segment"),
        P("segment", None),
        P(None, None, "seq", "segment"),
    )
    return jax.shard_map(
        per_device,
        mesh=mesh,
        in_specs=placed,
        out_specs=(P("seq", "segment"), P("seq", "segment")),
        check_vma=False,
    )
```

```python
import jax
import jax.numpy as jnp
from jax import lax
from jax.experimental import pallas as pl
from jax.experimental.pallas import tpu as pltpu
from jax.sharding import PartitionSpec as P

HD = 128
SECT = 8
CH = 64
NEIGH = 2
NBL = 128
TICKS = 2


EPS = 1e-05


def swapped(block, axis, apart):
    count = lax.axis_size(axis)
    route = []
    for low in range(count):
        high = low | 1 << apart
        if high != low and high < count:
            route += [(low, high), (high, low)]
    return lax.ppermute(block, axis, route)


def passed_along(block, axis, distance):
    devices = range(lax.axis_size(axis))
    route = [(i - distance, i) for i in devices if i - distance in devices]
    return lax.ppermute(block, axis, route)


def assemble(piece, head_group, bit_order, total_bits):
    current = piece
    for bit_index in bit_order:
        other = swapped(current, "segment", bit_index)
        is_upper = head_group // 2**bit_index % 2 == 1
        lower_half = jnp.where(is_upper, other, current)
        upper_half = jnp.where(is_upper, current, other)
        current = jnp.stack([lower_half, upper_half], axis=1)
    count_bits = len(bit_order)
    permutation = [0]
    for target in range(count_bits):
        wanted = total_bits - 1 - target
        permutation.append(1 + (count_bits - 1 - bit_order.index(wanted)))
    permutation.append(count_bits + 1)
    if count_bits > 0:
        current = jnp.transpose(current, permutation)
    return current.reshape(piece.shape[0], -1)


def share_sums(term, head_group, bit_order, total_bits):
    partial_value = term.astype(jnp.float32)
    tok_rows = partial_value.shape[0]
    current = partial_value.reshape(
        (tok_rows,) + (2,) * total_bits + (partial_value.shape[1] // 2**total_bits,)
    )
    remaining = list(range(total_bits - 1, -1, -1))
    for bit_index in bit_order:
        axis_pos = 1 + remaining.index(bit_index)
        lower_half = lax.index_in_dim(current, 0, axis_pos, keepdims=False)
        upper_half = lax.index_in_dim(current, 1, axis_pos, keepdims=False)
        is_upper = head_group // 2**bit_index % 2 == 1
        kept_half = jnp.where(is_upper, upper_half, lower_half)
        sent_half = jnp.where(is_upper, lower_half, upper_half)
        current = kept_half + swapped(sent_half.astype(jnp.bfloat16), "segment", bit_index).astype(
            sent_half.dtype
        )
        remaining = [bit_left for bit_left in remaining if bit_left != bit_index]
    return current


def local_layer(whole, keys_values, edge_kv, w_query, w_out):
    wide = whole.astype(jnp.float32)
    normed = (wide * lax.rsqrt(jnp.mean(wide * wide, axis=-1, keepdims=True) + EPS)).astype(
        jnp.bfloat16
    )
    queries = jnp.dot(normed, w_query, preferred_element_type=jnp.float32).astype(jnp.bfloat16)
    tokens = queries.shape[0]
    head_cols = queries.shape[1]
    groups = tokens // CH + 1
    padded = jnp.concatenate(
        [
            jnp.zeros((1, head_cols), jnp.bfloat16),
            queries,
            jnp.zeros((CH - 1, head_cols), jnp.bfloat16),
        ],
        axis=0,
    )
    padded = padded.reshape(groups, CH, head_cols // HD, HD)
    extended = jnp.concatenate([edge_kv, keys_values], axis=1).reshape(
        2, groups, NEIGH * NBL, head_cols // HD, HD
    )
    scores = jnp.einsum(
        "gchd,gkhd->ghck", padded, extended[0], preferred_element_type=jnp.float32
    ) * HD ** (-0.5)
    exponent = jnp.exp(scores)
    weights = (exponent / jnp.sum(exponent, axis=-1, keepdims=True)).astype(jnp.bfloat16)
    attended = jnp.einsum(
        "ghck,gkhd->gchd", weights, extended[1], preferred_element_type=jnp.float32
    ).astype(jnp.bfloat16)
    attended = attended.reshape(-1, head_cols)[1 : 1 + tokens]
    term = jnp.dot(attended, w_out, preferred_element_type=jnp.float32).astype(jnp.bfloat16)
    return lax.optimization_barrier(term)


MESH = pl.DeviceIdType.MESH
LAG = 3
TAIL = 16
AHEAD = 4


def relay_kernel(
    x_hbm, wq_hbm, wo_hbm, kv_hbm, first_hbm, second_hbm,
    x_v, wq_v, wo_v, kv_v, x2_v, y_v, y2_v, acc_v, q_v, hq_v, ha_v, la_v, lb_v, att_v, r_v,
    x_sem, wq_sem, wo_sem, kv_sem, hq_send, hq_recv, ha_send, ha_recv,
    rel_send, rel_recv, out_sem,
):
    nq, width, cw = wq_v.shape
    nf, cols, fw = wo_v.shape
    keys = kv_v.shape[3]
    half = keys // 2
    k, s = lax.axis_index("seq"), lax.axis_index("segment")
    nk, ns = lax.axis_size("seq"), lax.axis_size("segment")
    has_prev, has_next = k > 0, k < nk - 1
    has_in, has_out = s > 0, s < ns - 1
    prev = (lax.rem(k + nk - 1, nk), s)
    following = (lax.rem(k + 1, nk), s)
    below = (k, lax.rem(s + ns - 1, ns))
    above = (k, lax.rem(s + 1, ns))
    top, low = pl.ds(0, CH), pl.ds(CH, CH)
    last_row = lax.broadcasted_iota(jnp.int32, (CH, cw), 0) == CH - 1

    def head_cols(n):
        return pl.ds(pl.multiple_of(n * cw, cw), cw)

    def feature_cols(c):
        return pl.ds(pl.multiple_of(c * fw, fw), fw)

    def load_wq(c):
        return pltpu.make_async_copy(wq_hbm.at[:, head_cols(c)], wq_v.at[c], wq_sem.at[c])

    def load_kv(t, c):
        return pltpu.make_async_copy(
            kv_hbm.at[t, :, :, head_cols(c)], kv_v.at[t, c], kv_sem.at[t, c]
        )

    def load_wo(c):
        return pltpu.make_async_copy(wo_hbm.at[:, feature_cols(c)], wo_v.at[c], wo_sem.at[c])

    def halo_q(t, n):
        return pltpu.make_async_remote_copy(
            src_ref=q_v.at[t, n, top], dst_ref=hq_v.at[t, n],
            send_sem=hq_send.at[t, n], recv_sem=hq_recv.at[t, n],
            device_id=prev, device_id_type=MESH,
        )

    def halo_a(t, n):
        return pltpu.make_async_remote_copy(
            src_ref=ha_v.at[t, n], dst_ref=att_v.at[t, top, head_cols(n)],
            send_sem=ha_send.at[t, n], recv_sem=ha_recv.at[t, n],
            device_id=following, device_id_type=MESH,
        )

    parts = (pl.ds(0, CH), pl.ds(2 * CH - TAIL, TAIL), pl.ds(CH, CH - TAIL))

    def relay(b, c):
        rows = parts[b]
        return pltpu.make_async_remote_copy(
            src_ref=y_v.at[c, rows], dst_ref=x2_v.at[c, rows],
            send_sem=rel_send.at[b, c], recv_sem=rel_recv.at[b, c],
            device_id=above, device_id_type=MESH,
        )

    def store(t, c):
        buffer, target = ((y_v, first_hbm), (y2_v, second_hbm))[t]
        return pltpu.make_async_copy(
            buffer.at[c], target.at[:, feature_cols(c)], out_sem.at[t, c]
        )

    ones = jnp.ones((half, HD), jnp.bfloat16)

    def attend(block, t, n, span):
        at_keys = pl.ds(span * half, half)
        heads = []
        for h in range(cw // HD):
            at = slice(h * HD, (h + 1) * HD)
            scores = lax.dot_general(
                block[:, at], kv_v[t, n, 0, at_keys, at], (((1,), (1,)), ((), ())),
                preferred_element_type=jnp.float32,
            )
            most = jnp.max(scores, axis=1, keepdims=True)
            exponent = jnp.exp((scores - most) * HD ** (-0.5)).astype(jnp.bfloat16)
            values = jnp.concatenate([kv_v[t, n, 1, at_keys, at], ones], axis=1)
            both = jnp.dot(exponent, values, preferred_element_type=jnp.float32)
            heads.append(both[:, :HD] / both[:, HD:])
        return jnp.concatenate(heads, axis=1).astype(jnp.bfloat16)

    def loop(start, stop, body):
        def step(i, carry):
            body(i)
            return carry

        lax.fori_loop(start, stop, step, 0)

    load_x = pltpu.make_async_copy(x_hbm, x_v, x_sem)
    load_x.start()
    for c in range(AHEAD):
        load_wq(c).start()
        load_kv(0, c).start()

    barrier = pltpu.get_barrier_semaphore()
    pairs = ((has_prev, prev), (has_next, following), (has_in, below), (has_out, above))
    for exists, device in pairs:

        @pl.when(exists)
        def _(device=device):
            pl.semaphore_signal(barrier, inc=1, device_id=device, device_id_type=MESH)

    @pl.when(jnp.logical_not(has_next))
    def _():
        hq_v[...] = jnp.zeros_like(hq_v)

    @pl.when(jnp.logical_not(has_prev))
    def _():
        att_v[:, top, :] = jnp.zeros_like(att_v[:, top, :])

    @pl.when(jnp.logical_not(has_in))
    def _():
        x2_v[...] = jnp.zeros_like(x2_v)

    acc_v[...] = jnp.zeros_like(acc_v)
    load_x.wait()
    wide = x_v[...].astype(jnp.float32)
    scale = lax.rsqrt(jnp.mean(wide * wide, axis=1, keepdims=True) + EPS)
    r_v[...] = jnp.broadcast_to(scale, r_v.shape)
    pl.semaphore_wait(barrier, sum(exists.astype(jnp.int32) for exists, _ in pairs))

    def keep_own(t, n, out):
        at = head_cols(n)
        att_v[t, low, at] = out
        la_v[:, at] = out[CH - TAIL:]

    def keep_halo(t, n, out):
        ha_v[t, n] = out
        lb_v[:, head_cols(n)] = out[CH - TAIL:]

    def send_halo(t, n):
        @pl.when(has_next)
        def _():
            halo_a(t, n).start()

    def await_halo(t, n):
        @pl.when(has_next)
        def _():
            halo_q(t, n).wait_recv()

    def join(t):
        @pl.when(has_prev)
        def _():
            loop(0, nq, lambda n: halo_a(t, n).wait_recv())

        end = lax.broadcasted_iota(jnp.int32, la_v.shape, 0) == TAIL - 1
        top_end, low_end = pl.ds(CH - TAIL, TAIL), pl.ds(2 * CH - TAIL, TAIL)
        att_v[t, top_end] = jnp.where(end, la_v[...], att_v[t, top_end])
        att_v[t, low_end] = jnp.where(end, lb_v[...], att_v[t, low_end])

    def step(c, with_q, own, others):
        if with_q:
            load_wq(c).wait()

            @pl.when(c + AHEAD < nq)
            def _():
                load_wq(c + AHEAD).start()
                load_kv(0, c + AHEAD).start()

            @pl.when(c + AHEAD >= nq)
            def _():
                load_wo(c + AHEAD - nq).start()

        if own is not None:
            load_kv(0, own).wait()
        for n in others:
            await_halo(0, n)
        if own is not None:
            own_block = jnp.where(last_row, q_v[0, own, top], q_v[0, own, low])
        blocks = [jnp.where(last_row, q_v[0, n, low], hq_v[0, n]) for n in others]
        if with_q:
            total = jnp.dot(x_v[...], wq_v[c], preferred_element_type=jnp.float32)
            made = (total * r_v[:, :1]).astype(jnp.bfloat16)
        if own is not None:
            own_out = attend(own_block, 0, own, 0)
        outs = [attend(block, 0, n, 1) for n, block in zip(others, blocks)]
        if with_q:
            q_v[0, c] = made

            @pl.when(has_prev)
            def _():
                halo_q(0, c).start()

        for n, out in zip(others, outs):
            keep_halo(0, n, out)
            send_halo(0, n)
        if own is not None:
            keep_own(0, own, own_out)

    step(0, True, None, [])
    loop(1, LAG, lambda c: step(c, True, c - 1, []))
    loop(LAG, nq, lambda c: step(c, True, c - 1, [c - LAG]))
    for c in range(AHEAD, nf):
        load_wo(c).start()
    step(nq, False, nq - 1, [nq - 3, nq - 2])
    step(nq, False, None, [nq - 1])
    join(0)

    def project(t, c):
        term = jnp.dot(att_v[t], wo_v[c], preferred_element_type=jnp.float32)
        return term.astype(jnp.bfloat16).astype(jnp.float32)

    def first_chunk(c):
        load_wo(c).wait()
        load_kv(1, c).start()
        y_v[c] = (x_v[:, feature_cols(c)].astype(jnp.float32) + project(0, c)).astype(jnp.bfloat16)

        @pl.when(has_out)
        def _():
            relay(0, c).start()
            relay(1, c).start()

        store(0, c).start()

    loop(0, nf, first_chunk)

    @pl.when(has_out)
    def _():
        loop(0, nf, lambda c: relay(2, c).start())

    def gather_early(c):
        @pl.when(has_in)
        def _():
            relay(0, c).wait_recv()
            relay(1, c).wait_recv()

        block = jnp.concatenate([x2_v[c, parts[0]], x2_v[c, parts[1]]], axis=0)
        for n in range(nq):
            made = jnp.dot(block, wq_v[n, feature_cols(c), :], preferred_element_type=jnp.float32)
            acc_v[n, parts[0]] += made[:CH]
            acc_v[n, parts[1]] += made[CH:]

    def scale_rows(rows):
        squares = jnp.zeros((rows.size, 1), jnp.float32)
        for c in range(nf):
            block = x2_v[c, rows].astype(jnp.float32)
            squares += jnp.sum(block * block, axis=1, keepdims=True)
        return lax.rsqrt(squares / width + EPS)

    loop(0, nf, gather_early)
    for rows in parts[:2]:
        scale = scale_rows(rows)
        for n in range(nq):
            q_v[1, n, rows] = (acc_v[n, rows] * scale).astype(jnp.bfloat16)

    @pl.when(has_prev)
    def _():
        loop(0, nq, lambda n: halo_q(1, n).start())

    loop(0, nq, lambda n: load_kv(1, n).wait())

    def attend_halo(n):
        return attend(jnp.where(last_row, q_v[1, n, low], hq_v[1, n]), 1, n, 1)

    def gather_late(c, with_halo):
        other = c - LAG

        @pl.when(has_in)
        def _():
            relay(2, c).wait_recv()

        if with_halo:
            await_halo(1, other)
            out = attend_halo(other)
        block = x2_v[c, parts[2]]
        for n in range(nq):
            acc_v[n, parts[2]] += jnp.dot(
                block, wq_v[n, feature_cols(c), :], preferred_element_type=jnp.float32
            )
        if with_halo:
            keep_halo(1, other, out)
            send_halo(1, other)

    q_v[1, :, parts[2]] = jnp.zeros_like(q_v[1, :, parts[2]])
    loop(0, LAG, lambda c: gather_late(c, False))
    loop(LAG, nq, lambda c: gather_late(c, True))
    rest = range(nq - LAG, nq)
    for n in rest:
        await_halo(1, n)
    outs = [attend_halo(n) for n in rest]
    for n, out in zip(rest, outs):
        keep_halo(1, n, out)
        send_halo(1, n)
    r_v[parts[2]] = jnp.broadcast_to(scale_rows(parts[2]), (CH - TAIL, r_v.shape[1]))

    def finish(group):
        outs = []
        for i in range(4):
            n = 4 * group + i
            late = (acc_v[n, parts[2]] * r_v[parts[2], :1]).astype(jnp.bfloat16)
            mine = jnp.concatenate([late, q_v[1, n, parts[1]]], axis=0)
            outs.append(attend(jnp.where(last_row, q_v[1, n, top], mine), 1, n, 0))
        for i, out in enumerate(outs):
            keep_own(1, 4 * group + i, out)

    loop(0, nq // 4, finish)
    join(1)

    def second_chunk(c):
        y2_v[c] = (x2_v[c].astype(jnp.float32) + project(1, c)).astype(jnp.bfloat16)
        store(1, c).start()

    loop(0, nf, second_chunk)

    @pl.when(has_prev)
    def _():
        for t in range(TICKS):
            loop(0, nq, lambda n: halo_q(t, n).wait_send())

    @pl.when(has_next)
    def _():
        for t in range(TICKS):
            loop(0, nq, lambda n: halo_a(t, n).wait_send())

    @pl.when(has_out)
    def _():
        for b in range(3):
            loop(0, nf, lambda c: relay(b, c).wait_send())

    for t in range(TICKS):
        loop(0, nf, lambda c: store(t, c).wait())


def relay_call(stream, w_query, w_out, neighbour_kv):
    rows, width = stream.shape
    cols = w_query.shape[1]
    keys = neighbour_kv.shape[2]
    cw = 2 * HD
    nq = cols // cw
    fw = width // nq
    bf16, dma = jnp.bfloat16, pltpu.SemaphoreType.DMA
    hbm = pl.BlockSpec(memory_space=pl.ANY)
    flops = TICKS * 2 * rows * cols * (2 * width + 4 * keys)
    read = 2 * (stream.size + w_query.size + w_out.size + neighbour_kv.size + 2 * stream.size)
    return pl.pallas_call(
        relay_kernel,
        out_shape=[jax.ShapeDtypeStruct(stream.shape, bf16)] * 2,
        in_specs=[hbm] * 4,
        out_specs=[hbm] * 2,
        scratch_shapes=[
            pltpu.VMEM((rows, width), bf16),
            pltpu.VMEM((nq, width, cw), bf16),
            pltpu.VMEM((nq, cols, fw), bf16),
            pltpu.VMEM((TICKS, nq, 2, keys, cw), bf16),
            pltpu.VMEM((nq, rows, fw), bf16),
            pltpu.VMEM((nq, rows, fw), bf16),
            pltpu.VMEM((nq, rows, fw), bf16),
            pltpu.VMEM((nq, rows, cw), jnp.float32),
            pltpu.VMEM((TICKS, nq, rows, cw), bf16),
            pltpu.VMEM((TICKS, nq, CH, cw), bf16),
            pltpu.VMEM((TICKS, nq, CH, cw), bf16),
            pltpu.VMEM((TAIL, cols), bf16),
            pltpu.VMEM((TAIL, cols), bf16),
            pltpu.VMEM((TICKS, rows, cols), bf16),
            pltpu.VMEM((rows, 128), jnp.float32),
            dma,
            dma((nq,)),
            dma((nq,)),
            dma((TICKS, nq)),
            dma((TICKS, nq)),
            dma((TICKS, nq)),
            dma((TICKS, nq)),
            dma((TICKS, nq)),
            dma((3, nq)),
            dma((3, nq)),
            dma((TICKS, nq)),
        ],
        compiler_params=pltpu.CompilerParams(
            collective_id=0, has_side_effects=True, vmem_limit_bytes=60 * 2**20
        ),
        cost_estimate=pl.CostEstimate(flops=flops, bytes_accessed=read, transcendentals=0),
    )(stream, w_query, w_out, neighbour_kv)


def copy_kernel(first_in, second_in, first_out, second_out, sem):
    copies = []
    for i, (source, target) in enumerate(((first_in, first_out), (second_in, second_out))):
        rows = source.shape[0] // sem.shape[1]
        for j in range(sem.shape[1]):
            at = pl.ds(j * rows, rows)
            copies.append(pltpu.make_async_copy(source.at[at], target.at[at], sem.at[i, j]))
    for copy in copies:
        copy.start()
    for copy in copies:
        copy.wait()


def copied(first, second):
    hbm = pl.BlockSpec(memory_space=pl.ANY)
    return pl.pallas_call(
        copy_kernel,
        out_shape=[jax.ShapeDtypeStruct(a.shape, a.dtype) for a in (first, second)],
        in_specs=[hbm] * 2,
        out_specs=[hbm] * 2,
        scratch_shapes=[pltpu.SemaphoreType.DMA((2, 4))],
        compiler_params=pltpu.CompilerParams(vmem_limit_bytes=60 * 2**20),
        cost_estimate=pl.CostEstimate(flops=0, bytes_accessed=8 * first.size, transcendentals=0),
    )(first, second)


def fits(stream, w_query, neighbour_kv):
    rows, width = stream.shape
    cols = w_query.shape[1]
    return (
        lax.axis_size("segment") == SECT
        and rows == 2 * CH
        and neighbour_kv.shape[2] == 2 * NEIGH * NBL
        and cols % (8 * HD) == 0
        and width % (cols // (2 * HD) * 128) == 0
        and cols // (2 * HD) >= AHEAD
        and 2 * width * cols * 2 + neighbour_kv.size * 2 <= 42 * 2**20
    )


def per_device(stream, w_query, w_out, neighbour_kv):
    if fits(stream, w_query, neighbour_kv):
        return tuple(copied(*relay_call(stream, w_query, w_out, neighbour_kv)))
    groups_per = lax.axis_size("segment") // SECT
    head_group = lax.axis_index("segment") % groups_per
    total_bits = groups_per.bit_length() - 1
    bit_order = list(range(total_bits))
    edge_rows = NEIGH * NBL
    edges = passed_along(neighbour_kv[:, :, neighbour_kv.shape[2] - edge_rows :, :], "seq", 1)
    current = stream
    whole = assemble(current, head_group, bit_order, total_bits)
    outputs = []
    for tick_no in range(TICKS):
        term = local_layer(whole, neighbour_kv[tick_no], edges[tick_no], w_query, w_out)
        summed = share_sums(term, head_group, bit_order, total_bits)
        result = (current.astype(jnp.float32) + summed).astype(jnp.bfloat16)
        outputs.append(result)
        if tick_no + 1 < TICKS:
            current = passed_along(result, "segment", groups_per)
            whole = assemble(current, head_group, bit_order, total_bits)
    return (outputs[0], outputs[TICKS - 1])


def solution(mesh):
    placed = (
        P("seq", "segment"),
        P(None, "segment"),
        P("segment", None),
        P(None, None, "seq", "segment"),
    )
    return jax.shard_map(
        per_device,
        mesh=mesh,
        in_specs=placed,
        out_specs=(P("seq", "segment"), P("seq", "segment")),
        check_vma=False,
    )
```

```python
import jax
import jax.numpy as jnp
from jax import lax
from jax.experimental import pallas as pl
from jax.experimental.pallas import tpu as pltpu
from jax.sharding import PartitionSpec as P

HD = 128
SECT = 8
CH = 64
NEIGH = 2
NBL = 128
TICKS = 2


EPS = 1e-05


def swapped(block, axis, apart):
    count = lax.axis_size(axis)
    route = []
    for low in range(count):
        high = low | 1 << apart
        if high != low and high < count:
            route += [(low, high), (high, low)]
    return lax.ppermute(block, axis, route)


def passed_along(block, axis, distance):
    devices = range(lax.axis_size(axis))
    route = [(i - distance, i) for i in devices if i - distance in devices]
    return lax.ppermute(block, axis, route)


def assemble(piece, head_group, bit_order, total_bits):
    current = piece
    for bit_index in bit_order:
        other = swapped(current, "segment", bit_index)
        is_upper = head_group // 2**bit_index % 2 == 1
        lower_half = jnp.where(is_upper, other, current)
        upper_half = jnp.where(is_upper, current, other)
        current = jnp.stack([lower_half, upper_half], axis=1)
    count_bits = len(bit_order)
    permutation = [0]
    for target in range(count_bits):
        wanted = total_bits - 1 - target
        permutation.append(1 + (count_bits - 1 - bit_order.index(wanted)))
    permutation.append(count_bits + 1)
    if count_bits > 0:
        current = jnp.transpose(current, permutation)
    return current.reshape(piece.shape[0], -1)


def share_sums(term, head_group, bit_order, total_bits):
    partial_value = term.astype(jnp.float32)
    tok_rows = partial_value.shape[0]
    current = partial_value.reshape(
        (tok_rows,) + (2,) * total_bits + (partial_value.shape[1] // 2**total_bits,)
    )
    remaining = list(range(total_bits - 1, -1, -1))
    for bit_index in bit_order:
        axis_pos = 1 + remaining.index(bit_index)
        lower_half = lax.index_in_dim(current, 0, axis_pos, keepdims=False)
        upper_half = lax.index_in_dim(current, 1, axis_pos, keepdims=False)
        is_upper = head_group // 2**bit_index % 2 == 1
        kept_half = jnp.where(is_upper, upper_half, lower_half)
        sent_half = jnp.where(is_upper, lower_half, upper_half)
        current = kept_half + swapped(sent_half.astype(jnp.bfloat16), "segment", bit_index).astype(
            sent_half.dtype
        )
        remaining = [bit_left for bit_left in remaining if bit_left != bit_index]
    return current


def local_layer(whole, keys_values, edge_kv, w_query, w_out):
    wide = whole.astype(jnp.float32)
    normed = (wide * lax.rsqrt(jnp.mean(wide * wide, axis=-1, keepdims=True) + EPS)).astype(
        jnp.bfloat16
    )
    queries = jnp.dot(normed, w_query, preferred_element_type=jnp.float32).astype(jnp.bfloat16)
    tokens = queries.shape[0]
    head_cols = queries.shape[1]
    groups = tokens // CH + 1
    padded = jnp.concatenate(
        [
            jnp.zeros((1, head_cols), jnp.bfloat16),
            queries,
            jnp.zeros((CH - 1, head_cols), jnp.bfloat16),
        ],
        axis=0,
    )
    padded = padded.reshape(groups, CH, head_cols // HD, HD)
    extended = jnp.concatenate([edge_kv, keys_values], axis=1).reshape(
        2, groups, NEIGH * NBL, head_cols // HD, HD
    )
    scores = jnp.einsum(
        "gchd,gkhd->ghck", padded, extended[0], preferred_element_type=jnp.float32
    ) * HD ** (-0.5)
    exponent = jnp.exp(scores)
    weights = (exponent / jnp.sum(exponent, axis=-1, keepdims=True)).astype(jnp.bfloat16)
    attended = jnp.einsum(
        "ghck,gkhd->gchd", weights, extended[1], preferred_element_type=jnp.float32
    ).astype(jnp.bfloat16)
    attended = attended.reshape(-1, head_cols)[1 : 1 + tokens]
    term = jnp.dot(attended, w_out, preferred_element_type=jnp.float32).astype(jnp.bfloat16)
    return lax.optimization_barrier(term)


MESH = pl.DeviceIdType.MESH
LAG = 3
DELAY = 3
LATE = 5
TAIL = 16
AHEAD = 4


def relay_kernel(
    x_hbm, wq_hbm, wo_hbm, kv_hbm, first_hbm, second_hbm,
    x_v, wq_v, wo_v, kv_v, x2_v, y_v, y2_v, acc_v, q_v, hq_v, ha_v, la_v, lb_v, att_v, r_v,
    x_sem, wq_sem, wo_sem, kv_sem, hq_send, hq_recv, ha_send, ha_recv,
    rel_send, rel_recv, out_sem,
):
    nq, width, cw = wq_v.shape
    nf, cols, fw = wo_v.shape
    keys = kv_v.shape[3]
    half = keys // 2
    k, s = lax.axis_index("seq"), lax.axis_index("segment")
    nk, ns = lax.axis_size("seq"), lax.axis_size("segment")
    has_prev, has_next = k > 0, k < nk - 1
    has_in, has_out = s > 0, s < ns - 1
    prev = (lax.rem(k + nk - 1, nk), s)
    following = (lax.rem(k + 1, nk), s)
    below = (k, lax.rem(s + ns - 1, ns))
    above = (k, lax.rem(s + 1, ns))
    top, low = pl.ds(0, CH), pl.ds(CH, CH)
    last_row = lax.broadcasted_iota(jnp.int32, (CH, cw), 0) == CH - 1

    def head_cols(n):
        return pl.ds(pl.multiple_of(n * cw, cw), cw)

    def feature_cols(c):
        return pl.ds(pl.multiple_of(c * fw, fw), fw)

    def load_wq(c):
        return pltpu.make_async_copy(wq_hbm.at[:, head_cols(c)], wq_v.at[c], wq_sem.at[c])

    def load_kv(t, c):
        return pltpu.make_async_copy(
            kv_hbm.at[t, :, :, head_cols(c)], kv_v.at[t, c], kv_sem.at[t, c]
        )

    def load_wo(c):
        return pltpu.make_async_copy(wo_hbm.at[:, feature_cols(c)], wo_v.at[c], wo_sem.at[c])

    def halo_q(t, n):
        return pltpu.make_async_remote_copy(
            src_ref=q_v.at[t, n, top], dst_ref=hq_v.at[t, n],
            send_sem=hq_send.at[t, n], recv_sem=hq_recv.at[t, n],
            device_id=prev, device_id_type=MESH,
        )

    def halo_a(t, n):
        return pltpu.make_async_remote_copy(
            src_ref=ha_v.at[t, n], dst_ref=att_v.at[t, top, head_cols(n)],
            send_sem=ha_send.at[t, n], recv_sem=ha_recv.at[t, n],
            device_id=following, device_id_type=MESH,
        )

    parts = (pl.ds(0, CH), pl.ds(2 * CH - TAIL, TAIL), pl.ds(CH, CH - TAIL))

    def relay(b, c):
        rows = parts[b]
        return pltpu.make_async_remote_copy(
            src_ref=y_v.at[c, rows], dst_ref=x2_v.at[c, rows],
            send_sem=rel_send.at[b, c], recv_sem=rel_recv.at[b, c],
            device_id=above, device_id_type=MESH,
        )

    def store(t, c):
        buffer, target = ((y_v, first_hbm), (y2_v, second_hbm))[t]
        return pltpu.make_async_copy(
            buffer.at[c], target.at[:, feature_cols(c)], out_sem.at[t, c]
        )

    ones = jnp.ones((half, HD), jnp.bfloat16)

    def attend(block, t, n, span):
        at_keys = pl.ds(span * half, half)
        heads = []
        for h in range(cw // HD):
            at = slice(h * HD, (h + 1) * HD)
            scores = lax.dot_general(
                block[:, at], kv_v[t, n, 0, at_keys, at], (((1,), (1,)), ((), ())),
                preferred_element_type=jnp.float32,
            )
            most = jnp.max(scores, axis=1, keepdims=True)
            exponent = jnp.exp((scores - most) * HD ** (-0.5)).astype(jnp.bfloat16)
            values = jnp.concatenate([kv_v[t, n, 1, at_keys, at], ones], axis=1)
            both = jnp.dot(exponent, values, preferred_element_type=jnp.float32)
            heads.append(both[:, :HD] / both[:, HD:])
        return jnp.concatenate(heads, axis=1).astype(jnp.bfloat16)

    def loop(start, stop, body):
        def step(i, carry):
            body(i)
            return carry

        lax.fori_loop(start, stop, step, 0)

    load_x = pltpu.make_async_copy(x_hbm, x_v, x_sem)
    load_x.start()
    for c in range(AHEAD):
        load_wq(c).start()
        load_kv(0, c).start()

    barrier = pltpu.get_barrier_semaphore()
    pairs = ((has_prev, prev), (has_next, following), (has_in, below), (has_out, above))
    for exists, device in pairs:

        @pl.when(exists)
        def _(device=device):
            pl.semaphore_signal(barrier, inc=1, device_id=device, device_id_type=MESH)

    @pl.when(jnp.logical_not(has_next))
    def _():
        hq_v[...] = jnp.zeros_like(hq_v)

    @pl.when(jnp.logical_not(has_prev))
    def _():
        att_v[:, top, :] = jnp.zeros_like(att_v[:, top, :])

    @pl.when(jnp.logical_not(has_in))
    def _():
        x2_v[...] = jnp.zeros_like(x2_v)

    acc_v[...] = jnp.zeros_like(acc_v)
    load_x.wait()
    wide = x_v[...].astype(jnp.float32)
    scale = lax.rsqrt(jnp.mean(wide * wide, axis=1, keepdims=True) + EPS)
    r_v[...] = jnp.broadcast_to(scale, r_v.shape)
    pl.semaphore_wait(barrier, sum(exists.astype(jnp.int32) for exists, _ in pairs))

    def keep_own(t, n, out):
        at = head_cols(n)
        att_v[t, low, at] = out
        la_v[:, at] = out[CH - TAIL:]

    def keep_halo(t, n, out):
        ha_v[t, n] = out
        lb_v[:, head_cols(n)] = out[CH - TAIL:]

    def send_halo(t, n):
        @pl.when(has_next)
        def _():
            halo_a(t, n).start()

    def await_halo(t, n):
        @pl.when(has_next)
        def _():
            halo_q(t, n).wait_recv()

    def join(t):
        @pl.when(has_prev)
        def _():
            loop(0, nq, lambda n: halo_a(t, n).wait_recv())

        end = lax.broadcasted_iota(jnp.int32, la_v.shape, 0) == TAIL - 1
        top_end, low_end = pl.ds(CH - TAIL, TAIL), pl.ds(2 * CH - TAIL, TAIL)
        att_v[t, top_end] = jnp.where(end, la_v[...], att_v[t, top_end])
        att_v[t, low_end] = jnp.where(end, lb_v[...], att_v[t, low_end])

    def step(c, with_q, own, others):
        if with_q:
            load_wq(c).wait()

            @pl.when(c + AHEAD < nq)
            def _():
                load_wq(c + AHEAD).start()
                load_kv(0, c + AHEAD).start()

            @pl.when(c + AHEAD >= nq)
            def _():
                load_wo(c + AHEAD - nq).start()

        if own is not None:
            load_kv(0, own).wait()
        for n in others:
            await_halo(0, n)
        if own is not None:
            own_block = jnp.where(last_row, q_v[0, own, top], q_v[0, own, low])
        blocks = [jnp.where(last_row, q_v[0, n, low], hq_v[0, n]) for n in others]
        if with_q:
            total = jnp.dot(x_v[...], wq_v[c], preferred_element_type=jnp.float32)
            made = (total * r_v[:, :1]).astype(jnp.bfloat16)
        if own is not None:
            own_out = attend(own_block, 0, own, 0)
        outs = [attend(block, 0, n, 1) for n, block in zip(others, blocks)]
        if with_q:
            q_v[0, c] = made

            @pl.when(has_prev)
            def _():
                halo_q(0, c).start()

        for n, out in zip(others, outs):
            keep_halo(0, n, out)
            send_halo(0, n)
        if own is not None:
            keep_own(0, own, own_out)

    step(0, True, None, [])
    loop(1, LAG, lambda c: step(c, True, c - 1, []))
    loop(LAG, nq, lambda c: step(c, True, c - 1, [c - LAG]))
    for c in range(AHEAD, nf):
        load_wo(c).start()
    step(nq, False, nq - 1, [nq - 3, nq - 2])
    step(nq, False, None, [nq - 1])
    join(0)

    def project(t, c):
        term = jnp.dot(att_v[t], wo_v[c], preferred_element_type=jnp.float32)
        return term.astype(jnp.bfloat16).astype(jnp.float32)

    def first_chunk(c, with_out, with_in):
        early = c - DELAY
        if with_out:
            load_wo(c).wait()
            load_kv(1, c).start()
        if with_in:

            @pl.when(has_in)
            def _():
                relay(0, early).wait_recv()
                relay(1, early).wait_recv()

            block = jnp.concatenate([x2_v[early, parts[0]], x2_v[early, parts[1]]], axis=0)
        if with_out:
            residual = x_v[:, feature_cols(c)].astype(jnp.float32)
            result = (residual + project(0, c)).astype(jnp.bfloat16)
        if with_in:
            at = feature_cols(early)
            made = [
                jnp.dot(block, wq_v[n, at, :], preferred_element_type=jnp.float32)
                for n in range(nq)
            ]
        if with_out:
            y_v[c] = result

            @pl.when(has_out)
            def _():
                relay(0, c).start()
                relay(1, c).start()

            store(0, c).start()
        if with_in:
            for n in range(nq):
                acc_v[n, parts[0]] += made[n][:CH]
                acc_v[n, parts[1]] += made[n][CH:]

    loop(0, DELAY, lambda c: first_chunk(c, True, False))
    loop(DELAY, nf, lambda c: first_chunk(c, True, True))

    @pl.when(has_out)
    def _():
        loop(0, nf, lambda c: relay(2, c).start())

    loop(nf, nf + DELAY, lambda c: first_chunk(c, False, True))

    def scale_rows(rows):
        squares = jnp.zeros((rows.size, 1), jnp.float32)
        for c in range(nf):
            block = x2_v[c, rows].astype(jnp.float32)
            squares += jnp.sum(block * block, axis=1, keepdims=True)
        return lax.rsqrt(squares / width + EPS)

    for rows in parts[:2]:
        scale = scale_rows(rows)
        for n in range(nq):
            q_v[1, n, rows] = (acc_v[n, rows] * scale).astype(jnp.bfloat16)

    @pl.when(has_prev)
    def _():
        loop(0, nq, lambda n: halo_q(1, n).start())

    loop(0, nq, lambda n: load_kv(1, n).wait())

    def attend_halo(n):
        return attend(jnp.where(last_row, q_v[1, n, low], hq_v[1, n]), 1, n, 1)

    def gather_late(c, with_halo):
        other = c - LATE

        @pl.when(has_in)
        def _():
            relay(2, c).wait_recv()

        if with_halo:
            await_halo(1, other)
            out = attend_halo(other)
        block = x2_v[c, parts[2]]
        for n in range(nq):
            acc_v[n, parts[2]] += jnp.dot(
                block, wq_v[n, feature_cols(c), :], preferred_element_type=jnp.float32
            )
        if with_halo:
            keep_halo(1, other, out)
            send_halo(1, other)

    q_v[1, :, parts[2]] = jnp.zeros_like(q_v[1, :, parts[2]])
    loop(0, LATE, lambda c: gather_late(c, False))
    loop(LATE, nf, lambda c: gather_late(c, True))
    r_v[parts[2]] = jnp.broadcast_to(scale_rows(parts[2]), (CH - TAIL, r_v.shape[1]))
    groups = nq // 2

    def finish(group):
        other = nq - LATE + group
        await_halo(1, other)
        halo_out = attend_halo(other)
        outs = []
        for i in range(2):
            n = 2 * group + i
            late = (acc_v[n, parts[2]] * r_v[parts[2], :1]).astype(jnp.bfloat16)
            mine = jnp.concatenate([late, q_v[1, n, parts[1]]], axis=0)
            outs.append(attend(jnp.where(last_row, q_v[1, n, top], mine), 1, n, 0))
        keep_halo(1, other, halo_out)
        send_halo(1, other)
        for i, out in enumerate(outs):
            keep_own(1, 2 * group + i, out)

    loop(0, groups, finish)
    for n in range(nq - LATE + groups, nq):
        await_halo(1, n)
        keep_halo(1, n, attend_halo(n))
        send_halo(1, n)
    join(1)

    def second_chunk(c):
        y2_v[c] = (x2_v[c].astype(jnp.float32) + project(1, c)).astype(jnp.bfloat16)
        store(1, c).start()

    loop(0, nf, second_chunk)

    @pl.when(has_prev)
    def _():
        for t in range(TICKS):
            loop(0, nq, lambda n: halo_q(t, n).wait_send())

    @pl.when(has_next)
    def _():
        for t in range(TICKS):
            loop(0, nq, lambda n: halo_a(t, n).wait_send())

    @pl.when(has_out)
    def _():
        for b in range(3):
            loop(0, nf, lambda c: relay(b, c).wait_send())

    for t in range(TICKS):
        loop(0, nf, lambda c: store(t, c).wait())


def relay_call(stream, w_query, w_out, neighbour_kv):
    rows, width = stream.shape
    cols = w_query.shape[1]
    keys = neighbour_kv.shape[2]
    cw = 2 * HD
    nq = cols // cw
    fw = width // nq
    bf16, dma = jnp.bfloat16, pltpu.SemaphoreType.DMA
    hbm = pl.BlockSpec(memory_space=pl.ANY)
    flops = TICKS * 2 * rows * cols * (2 * width + 4 * keys)
    read = 2 * (stream.size + w_query.size + w_out.size + neighbour_kv.size + 2 * stream.size)
    return pl.pallas_call(
        relay_kernel,
        out_shape=[jax.ShapeDtypeStruct(stream.shape, bf16)] * 2,
        in_specs=[hbm] * 4,
        out_specs=[hbm] * 2,
        scratch_shapes=[
            pltpu.VMEM((rows, width), bf16),
            pltpu.VMEM((nq, width, cw), bf16),
            pltpu.VMEM((nq, cols, fw), bf16),
            pltpu.VMEM((TICKS, nq, 2, keys, cw), bf16),
            pltpu.VMEM((nq, rows, fw), bf16),
            pltpu.VMEM((nq, rows, fw), bf16),
            pltpu.VMEM((nq, rows, fw), bf16),
            pltpu.VMEM((nq, rows, cw), jnp.float32),
            pltpu.VMEM((TICKS, nq, rows, cw), bf16),
            pltpu.VMEM((TICKS, nq, CH, cw), bf16),
            pltpu.VMEM((TICKS, nq, CH, cw), bf16),
            pltpu.VMEM((TAIL, cols), bf16),
            pltpu.VMEM((TAIL, cols), bf16),
            pltpu.VMEM((TICKS, rows, cols), bf16),
            pltpu.VMEM((rows, 128), jnp.float32),
            dma,
            dma((nq,)),
            dma((nq,)),
            dma((TICKS, nq)),
            dma((TICKS, nq)),
            dma((TICKS, nq)),
            dma((TICKS, nq)),
            dma((TICKS, nq)),
            dma((3, nq)),
            dma((3, nq)),
            dma((TICKS, nq)),
        ],
        compiler_params=pltpu.CompilerParams(
            collective_id=0, has_side_effects=True, vmem_limit_bytes=60 * 2**20
        ),
        cost_estimate=pl.CostEstimate(flops=flops, bytes_accessed=read, transcendentals=0),
    )(stream, w_query, w_out, neighbour_kv)


def copy_kernel(first_in, second_in, first_out, second_out, held, in_sem, out_sem):
    moves = []
    for i, (source, target) in enumerate(((first_in, first_out), (second_in, second_out))):
        rows = source.shape[0] // in_sem.shape[1]
        for j in range(in_sem.shape[1]):
            at = pl.ds(j * rows, rows)
            fetch = pltpu.make_async_copy(source.at[at], held.at[i, at], in_sem.at[i, j])
            store = pltpu.make_async_copy(held.at[i, at], target.at[at], out_sem.at[i, j])
            fetch.start()
            moves.append((fetch, store))
    for fetch, store in moves:
        fetch.wait()
        store.start()
    for fetch, store in moves:
        store.wait()


def copied(first, second):
    hbm = pl.BlockSpec(memory_space=pl.ANY)
    return pl.pallas_call(
        copy_kernel,
        out_shape=[jax.ShapeDtypeStruct(a.shape, a.dtype) for a in (first, second)],
        in_specs=[hbm] * 2,
        out_specs=[hbm] * 2,
        scratch_shapes=[
            pltpu.VMEM((2,) + first.shape, first.dtype),
            pltpu.SemaphoreType.DMA((2, 4)),
            pltpu.SemaphoreType.DMA((2, 4)),
        ],
        compiler_params=pltpu.CompilerParams(vmem_limit_bytes=60 * 2**20),
        cost_estimate=pl.CostEstimate(flops=0, bytes_accessed=8 * first.size, transcendentals=0),
    )(first, second)


def fits(stream, w_query, neighbour_kv):
    rows, width = stream.shape
    cols = w_query.shape[1]
    return (
        lax.axis_size("segment") == SECT
        and rows == 2 * CH
        and neighbour_kv.shape[2] == 2 * NEIGH * NBL
        and cols % (8 * HD) == 0
        and width % (cols // (2 * HD) * 128) == 0
        and cols // (2 * HD) == 2 * AHEAD
        and 2 * width * cols * 2 + neighbour_kv.size * 2 <= 42 * 2**20
    )


def per_device(stream, w_query, w_out, neighbour_kv):
    if fits(stream, w_query, neighbour_kv):
        return tuple(copied(*relay_call(stream, w_query, w_out, neighbour_kv)))
    groups_per = lax.axis_size("segment") // SECT
    head_group = lax.axis_index("segment") % groups_per
    total_bits = groups_per.bit_length() - 1
    bit_order = list(range(total_bits))
    edge_rows = NEIGH * NBL
    edges = passed_along(neighbour_kv[:, :, neighbour_kv.shape[2] - edge_rows :, :], "seq", 1)
    current = stream
    whole = assemble(current, head_group, bit_order, total_bits)
    outputs = []
    for tick_no in range(TICKS):
        term = local_layer(whole, neighbour_kv[tick_no], edges[tick_no], w_query, w_out)
        summed = share_sums(term, head_group, bit_order, total_bits)
        result = (current.astype(jnp.float32) + summed).astype(jnp.bfloat16)
        outputs.append(result)
        if tick_no + 1 < TICKS:
            current = passed_along(result, "segment", groups_per)
            whole = assemble(current, head_group, bit_order, total_bits)
    return (outputs[0], outputs[TICKS - 1])


def solution(mesh):
    placed = (
        P("seq", "segment"),
        P(None, "segment"),
        P("segment", None),
        P(None, None, "seq", "segment"),
    )
    return jax.shard_map(
        per_device,
        mesh=mesh,
        in_specs=placed,
        out_specs=(P("seq", "segment"), P("seq", "segment")),
        check_vma=False,
    )
```

```python
import jax
import jax.numpy as jnp
from jax import lax
from jax.experimental import pallas as pl
from jax.experimental.pallas import tpu as pltpu
from jax.sharding import PartitionSpec as P

HD = 128
SECT = 8
CH = 64
NEIGH = 2
NBL = 128
TICKS = 2


EPS = 1e-05


def swapped(block, axis, apart):
    count = lax.axis_size(axis)
    route = []
    for low in range(count):
        high = low | 1 << apart
        if high != low and high < count:
            route += [(low, high), (high, low)]
    return lax.ppermute(block, axis, route)


def passed_along(block, axis, distance):
    devices = range(lax.axis_size(axis))
    route = [(i - distance, i) for i in devices if i - distance in devices]
    return lax.ppermute(block, axis, route)


def assemble(piece, head_group, bit_order, total_bits):
    current = piece
    for bit_index in bit_order:
        other = swapped(current, "segment", bit_index)
        is_upper = head_group // 2**bit_index % 2 == 1
        lower_half = jnp.where(is_upper, other, current)
        upper_half = jnp.where(is_upper, current, other)
        current = jnp.stack([lower_half, upper_half], axis=1)
    count_bits = len(bit_order)
    permutation = [0]
    for target in range(count_bits):
        wanted = total_bits - 1 - target
        permutation.append(1 + (count_bits - 1 - bit_order.index(wanted)))
    permutation.append(count_bits + 1)
    if count_bits > 0:
        current = jnp.transpose(current, permutation)
    return current.reshape(piece.shape[0], -1)


def share_sums(term, head_group, bit_order, total_bits):
    partial_value = term.astype(jnp.float32)
    tok_rows = partial_value.shape[0]
    current = partial_value.reshape(
        (tok_rows,) + (2,) * total_bits + (partial_value.shape[1] // 2**total_bits,)
    )
    remaining = list(range(total_bits - 1, -1, -1))
    for bit_index in bit_order:
        axis_pos = 1 + remaining.index(bit_index)
        lower_half = lax.index_in_dim(current, 0, axis_pos, keepdims=False)
        upper_half = lax.index_in_dim(current, 1, axis_pos, keepdims=False)
        is_upper = head_group // 2**bit_index % 2 == 1
        kept_half = jnp.where(is_upper, upper_half, lower_half)
        sent_half = jnp.where(is_upper, lower_half, upper_half)
        current = kept_half + swapped(sent_half.astype(jnp.bfloat16), "segment", bit_index).astype(
            sent_half.dtype
        )
        remaining = [bit_left for bit_left in remaining if bit_left != bit_index]
    return current


def local_layer(whole, keys_values, edge_kv, w_query, w_out):
    wide = whole.astype(jnp.float32)
    normed = (wide * lax.rsqrt(jnp.mean(wide * wide, axis=-1, keepdims=True) + EPS)).astype(
        jnp.bfloat16
    )
    queries = jnp.dot(normed, w_query, preferred_element_type=jnp.float32).astype(jnp.bfloat16)
    tokens = queries.shape[0]
    head_cols = queries.shape[1]
    groups = tokens // CH + 1
    padded = jnp.concatenate(
        [
            jnp.zeros((1, head_cols), jnp.bfloat16),
            queries,
            jnp.zeros((CH - 1, head_cols), jnp.bfloat16),
        ],
        axis=0,
    )
    padded = padded.reshape(groups, CH, head_cols // HD, HD)
    extended = jnp.concatenate([edge_kv, keys_values], axis=1).reshape(
        2, groups, NEIGH * NBL, head_cols // HD, HD
    )
    scores = jnp.einsum(
        "gchd,gkhd->ghck", padded, extended[0], preferred_element_type=jnp.float32
    ) * HD ** (-0.5)
    exponent = jnp.exp(scores)
    weights = (exponent / jnp.sum(exponent, axis=-1, keepdims=True)).astype(jnp.bfloat16)
    attended = jnp.einsum(
        "ghck,gkhd->gchd", weights, extended[1], preferred_element_type=jnp.float32
    ).astype(jnp.bfloat16)
    attended = attended.reshape(-1, head_cols)[1 : 1 + tokens]
    term = jnp.dot(attended, w_out, preferred_element_type=jnp.float32).astype(jnp.bfloat16)
    return lax.optimization_barrier(term)


MESH = pl.DeviceIdType.MESH
LAG = 3
DELAY = 3
LATE = 5
TAIL = 16
AHEAD = 4


def relay_kernel(
    x_hbm, wq_hbm, wo_hbm, kv_hbm, first_hbm, second_hbm,
    x_v, wq_v, wo_v, kv_v, x2_v, y_v, y2_v, acc_v, q_v, hq_v, ha_v, la_v, lb_v, att_v, r_v,
    x_sem, wq_sem, wo_sem, kv_sem, hq_send, hq_recv, ha_send, ha_recv,
    rel_send, rel_recv, out_sem,
):
    _, nq, _, cw = hq_v.shape
    nf, _, fw = y_v.shape
    halves, width, wide_cols = wq_v.shape
    quarters, cols, wide_features = wo_v.shape
    per_half, per_quarter = nq // halves, nf // quarters
    keys = kv_v.shape[2]
    half = keys // 2
    k, s = lax.axis_index("seq"), lax.axis_index("segment")
    nk, ns = lax.axis_size("seq"), lax.axis_size("segment")
    has_prev, has_next = k > 0, k < nk - 1
    has_in, has_out = s > 0, s < ns - 1
    prev = (lax.rem(k + nk - 1, nk), s)
    following = (lax.rem(k + 1, nk), s)
    below = (k, lax.rem(s + ns - 1, ns))
    above = (k, lax.rem(s + 1, ns))
    top, low = pl.ds(0, CH), pl.ds(CH, CH)
    last_row = lax.broadcasted_iota(jnp.int32, (CH, cw), 0) == CH - 1

    def head_cols(n):
        return pl.ds(pl.multiple_of(n * cw, cw), cw)

    def feature_cols(c):
        return pl.ds(pl.multiple_of(c * fw, fw), fw)

    wq_rows, wo_rows = width // AHEAD, cols // per_quarter

    def load_wq(h, j):
        at = pl.ds(j * wq_rows, wq_rows)
        source = wq_hbm.at[at, pl.ds(h * wide_cols, wide_cols)]
        return pltpu.make_async_copy(source, wq_v.at[h, at], wq_sem.at[h, j])

    def load_kv(t, i):
        which, at = i // AHEAD, pl.ds(i % AHEAD * (keys // AHEAD), keys // AHEAD)
        return pltpu.make_async_copy(
            kv_hbm.at[t, which, at], kv_v.at[t, which, at], kv_sem.at[t, i]
        )

    def load_wo(i):
        g, at = i // per_quarter, pl.ds(i % per_quarter * wo_rows, wo_rows)
        source = wo_hbm.at[at, pl.ds(g * wide_features, wide_features)]
        return pltpu.make_async_copy(source, wo_v.at[g, at], wo_sem.at[i])

    def await_wq(h):
        for j in range(AHEAD):
            load_wq(h, j).wait()
            if h + 1 < halves:
                load_wq(h + 1, j).start()
            else:
                load_wo(j).start()

    def halo_q(t, n):
        return pltpu.make_async_remote_copy(
            src_ref=q_v.at[t, n, top], dst_ref=hq_v.at[t, n],
            send_sem=hq_send.at[t, n], recv_sem=hq_recv.at[t, n],
            device_id=prev, device_id_type=MESH,
        )

    def halo_a(t, n):
        return pltpu.make_async_remote_copy(
            src_ref=ha_v.at[t, n], dst_ref=att_v.at[t, top, head_cols(n)],
            send_sem=ha_send.at[t, n], recv_sem=ha_recv.at[t, n],
            device_id=following, device_id_type=MESH,
        )

    parts = (pl.ds(0, CH), pl.ds(2 * CH - TAIL, TAIL), pl.ds(CH, CH - TAIL))

    def relay(b, c):
        rows = parts[b]
        return pltpu.make_async_remote_copy(
            src_ref=y_v.at[c, rows], dst_ref=x2_v.at[c, rows],
            send_sem=rel_send.at[b, c], recv_sem=rel_recv.at[b, c],
            device_id=above, device_id_type=MESH,
        )

    def store(t, c):
        buffer, target = ((y_v, first_hbm), (y2_v, second_hbm))[t]
        return pltpu.make_async_copy(
            buffer.at[c], target.at[:, feature_cols(c)], out_sem.at[t, c]
        )

    ones = jnp.ones((half, HD), jnp.bfloat16)

    def attend(block, t, n, span):
        at_keys = pl.ds(span * half, half)
        heads = []
        for h in range(cw // HD):
            at = pl.ds(pl.multiple_of(n * cw + h * HD, HD), HD)
            scores = lax.dot_general(
                block[:, h * HD:(h + 1) * HD], kv_v[t, 0, at_keys, at], (((1,), (1,)), ((), ())),
                preferred_element_type=jnp.float32,
            )
            most = jnp.max(scores, axis=1, keepdims=True)
            exponent = jnp.exp((scores - most) * HD ** (-0.5)).astype(jnp.bfloat16)
            values = jnp.concatenate([kv_v[t, 1, at_keys, at], ones], axis=1)
            both = jnp.dot(exponent, values, preferred_element_type=jnp.float32)
            heads.append(both[:, :HD] / both[:, HD:])
        return jnp.concatenate(heads, axis=1).astype(jnp.bfloat16)

    def loop(start, stop, body):
        def step(i, carry):
            body(i)
            return carry

        lax.fori_loop(start, stop, step, 0)

    load_x = pltpu.make_async_copy(x_hbm, x_v, x_sem)
    load_x.start()
    for j in range(AHEAD):
        load_wq(0, j).start()
    for i in range(2 * AHEAD):
        load_kv(0, i).start()

    barrier = pltpu.get_barrier_semaphore()
    pairs = ((has_prev, prev), (has_next, following), (has_in, below), (has_out, above))
    for exists, device in pairs:

        @pl.when(exists)
        def _(device=device):
            pl.semaphore_signal(barrier, inc=1, device_id=device, device_id_type=MESH)

    @pl.when(jnp.logical_not(has_next))
    def _():
        hq_v[...] = jnp.zeros_like(hq_v)

    @pl.when(jnp.logical_not(has_prev))
    def _():
        att_v[:, top, :] = jnp.zeros_like(att_v[:, top, :])

    @pl.when(jnp.logical_not(has_in))
    def _():
        x2_v[...] = jnp.zeros_like(x2_v)

    acc_v[...] = jnp.zeros_like(acc_v)
    load_x.wait()
    wide = x_v[...].astype(jnp.float32)
    scale = lax.rsqrt(jnp.mean(wide * wide, axis=1, keepdims=True) + EPS)
    r_v[...] = jnp.broadcast_to(scale, r_v.shape)
    pl.semaphore_wait(barrier, sum(exists.astype(jnp.int32) for exists, _ in pairs))

    def keep_own(t, n, out):
        at = head_cols(n)
        att_v[t, low, at] = out
        la_v[:, at] = out[CH - TAIL:]

    def keep_halo(t, n, out):
        ha_v[t, n] = out
        lb_v[:, head_cols(n)] = out[CH - TAIL:]

    def send_halo(t, n):
        @pl.when(has_next)
        def _():
            halo_a(t, n).start()

    def await_halo(t, n):
        @pl.when(has_next)
        def _():
            halo_q(t, n).wait_recv()

    def join(t):
        @pl.when(has_prev)
        def _():
            loop(0, nq, lambda n: halo_a(t, n).wait_recv())

        end = lax.broadcasted_iota(jnp.int32, la_v.shape, 0) == TAIL - 1
        top_end, low_end = pl.ds(CH - TAIL, TAIL), pl.ds(2 * CH - TAIL, TAIL)
        att_v[t, top_end] = jnp.where(end, la_v[...], att_v[t, top_end])
        att_v[t, low_end] = jnp.where(end, lb_v[...], att_v[t, low_end])

    def step(c, with_q, own, others):
        if with_q:
            for h in range(1, halves):

                @pl.when(c == h * per_half)
                def _():
                    await_wq(h)

        for n in others:
            await_halo(0, n)
        if own is not None:
            own_block = jnp.where(last_row, q_v[0, own, top], q_v[0, own, low])
        blocks = [jnp.where(last_row, q_v[0, n, low], hq_v[0, n]) for n in others]
        if with_q:
            at = pl.ds(pl.multiple_of(c % per_half * cw, cw), cw)
            weight = wq_v[c // per_half, :, at]
            total = jnp.dot(x_v[...], weight, preferred_element_type=jnp.float32)
            made = (total * r_v[:, :1]).astype(jnp.bfloat16)
        if own is not None:
            own_out = attend(own_block, 0, own, 0)
        outs = [attend(block, 0, n, 1) for n, block in zip(others, blocks)]
        if with_q:
            q_v[0, c] = made

            @pl.when(has_prev)
            def _():
                halo_q(0, c).start()

        for n, out in zip(others, outs):
            keep_halo(0, n, out)
            send_halo(0, n)
        if own is not None:
            keep_own(0, own, own_out)

    await_wq(0)
    step(0, True, None, [])
    for i in range(2 * AHEAD):
        load_kv(0, i).wait()
    loop(1, LAG, lambda c: step(c, True, c - 1, []))
    loop(LAG, nq, lambda c: step(c, True, c - 1, [c - LAG]))
    for c in range(AHEAD, nf):
        load_wo(c).start()
    step(nq, False, nq - 1, [nq - 3, nq - 2])
    step(nq, False, None, [nq - 1])
    join(0)

    def project(t, c):
        at = pl.ds(pl.multiple_of(c % per_quarter * fw, fw), fw)
        weight = wo_v[c // per_quarter, :, at]
        term = jnp.dot(att_v[t], weight, preferred_element_type=jnp.float32)
        return term.astype(jnp.bfloat16).astype(jnp.float32)

    def first_chunk(c, with_out, with_in):
        early = c - DELAY
        if with_out:

            @pl.when(c % per_quarter == 0)
            def _():
                for i in range(per_quarter):
                    load_wo(c + i).wait()

            load_kv(1, c).start()
        if with_in:

            @pl.when(has_in)
            def _():
                relay(0, early).wait_recv()
                relay(1, early).wait_recv()

            block = jnp.concatenate([x2_v[early, parts[0]], x2_v[early, parts[1]]], axis=0)
        if with_out:
            residual = x_v[:, feature_cols(c)].astype(jnp.float32)
            result = (residual + project(0, c)).astype(jnp.bfloat16)
        if with_in:
            at = feature_cols(early)
            made = [
                jnp.dot(block, wq_v[h, at, :], preferred_element_type=jnp.float32)
                for h in range(halves)
            ]
        if with_out:
            y_v[c] = result

            @pl.when(has_out)
            def _():
                relay(0, c).start()
                relay(1, c).start()

            store(0, c).start()
        if with_in:
            for h in range(halves):
                acc_v[h, parts[0]] += made[h][:CH]
                acc_v[h, parts[1]] += made[h][CH:]

    loop(0, DELAY, lambda c: first_chunk(c, True, False))
    loop(DELAY, nf, lambda c: first_chunk(c, True, True))

    @pl.when(has_out)
    def _():
        loop(0, nf, lambda c: relay(2, c).start())

    loop(nf, nf + DELAY, lambda c: first_chunk(c, False, True))

    def scale_rows(rows):
        squares = jnp.zeros((rows.size, 1), jnp.float32)
        for c in range(nf):
            block = x2_v[c, rows].astype(jnp.float32)
            squares += jnp.sum(block * block, axis=1, keepdims=True)
        return lax.rsqrt(squares / width + EPS)

    def make_queries(rows):
        scale = scale_rows(rows)
        for n in range(nq):
            at = pl.ds(n % per_half * cw, cw)
            q_v[1, n, rows] = (acc_v[n // per_half, rows, at] * scale).astype(jnp.bfloat16)

    for rows in parts[:2]:
        make_queries(rows)

    @pl.when(has_prev)
    def _():
        loop(0, nq, lambda n: halo_q(1, n).start())

    loop(0, nq, lambda n: load_kv(1, n).wait())

    def attend_halo(n):
        return attend(jnp.where(last_row, q_v[1, n, low], hq_v[1, n]), 1, n, 1)

    def gather_late(c, with_halo):
        other = c - LATE

        @pl.when(has_in)
        def _():
            relay(2, c).wait_recv()

        if with_halo:
            await_halo(1, other)
            out = attend_halo(other)
        block = x2_v[c, parts[2]]
        for h in range(halves):
            acc_v[h, parts[2]] += jnp.dot(
                block, wq_v[h, feature_cols(c), :], preferred_element_type=jnp.float32
            )
        if with_halo:
            keep_halo(1, other, out)
            send_halo(1, other)

    q_v[1, :, parts[2]] = jnp.zeros_like(q_v[1, :, parts[2]])
    loop(0, LATE, lambda c: gather_late(c, False))
    loop(LATE, nf, lambda c: gather_late(c, True))
    make_queries(parts[2])
    groups = nq // 2

    def finish(group):
        other = nq - LATE + group
        await_halo(1, other)
        halo_out = attend_halo(other)
        outs = []
        for i in range(2):
            n = 2 * group + i
            block = jnp.where(last_row, q_v[1, n, top], q_v[1, n, low])
            outs.append(attend(block, 1, n, 0))
        keep_halo(1, other, halo_out)
        send_halo(1, other)
        for i, out in enumerate(outs):
            keep_own(1, 2 * group + i, out)

    loop(0, groups, finish)
    for n in range(nq - LATE + groups, nq):
        await_halo(1, n)
        keep_halo(1, n, attend_halo(n))
        send_halo(1, n)
    join(1)

    def second_chunk(c):
        y2_v[c] = (x2_v[c].astype(jnp.float32) + project(1, c)).astype(jnp.bfloat16)
        store(1, c).start()

    loop(0, nf, second_chunk)

    @pl.when(has_prev)
    def _():
        for t in range(TICKS):
            loop(0, nq, lambda n: halo_q(t, n).wait_send())

    @pl.when(has_next)
    def _():
        for t in range(TICKS):
            loop(0, nq, lambda n: halo_a(t, n).wait_send())

    @pl.when(has_out)
    def _():
        for b in range(3):
            loop(0, nf, lambda c: relay(b, c).wait_send())

    for t in range(TICKS):
        loop(0, nf, lambda c: store(t, c).wait())


def relay_call(stream, w_query, w_out, neighbour_kv):
    rows, width = stream.shape
    cols = w_query.shape[1]
    keys = neighbour_kv.shape[2]
    cw = 2 * HD
    nq = cols // cw
    fw = width // nq
    bf16, dma = jnp.bfloat16, pltpu.SemaphoreType.DMA
    hbm = pl.BlockSpec(memory_space=pl.ANY)
    flops = TICKS * 2 * rows * cols * (2 * width + 4 * keys)
    read = 2 * (stream.size + w_query.size + w_out.size + neighbour_kv.size + 2 * stream.size)
    return pl.pallas_call(
        relay_kernel,
        out_shape=[jax.ShapeDtypeStruct(stream.shape, bf16)] * 2,
        in_specs=[hbm] * 4,
        out_specs=[hbm] * 2,
        scratch_shapes=[
            pltpu.VMEM((rows, width), bf16),
            pltpu.VMEM((2, width, cols // 2), bf16),
            pltpu.VMEM((4, cols, width // 4), bf16),
            pltpu.VMEM((TICKS, 2, keys, cols), bf16),
            pltpu.VMEM((nq, rows, fw), bf16),
            pltpu.VMEM((nq, rows, fw), bf16),
            pltpu.VMEM((nq, rows, fw), bf16),
            pltpu.VMEM((2, rows, cols // 2), jnp.float32),
            pltpu.VMEM((TICKS, nq, rows, cw), bf16),
            pltpu.VMEM((TICKS, nq, CH, cw), bf16),
            pltpu.VMEM((TICKS, nq, CH, cw), bf16),
            pltpu.VMEM((TAIL, cols), bf16),
            pltpu.VMEM((TAIL, cols), bf16),
            pltpu.VMEM((TICKS, rows, cols), bf16),
            pltpu.VMEM((rows, 128), jnp.float32),
            dma,
            dma((2, AHEAD)),
            dma((nq,)),
            dma((TICKS, nq)),
            dma((TICKS, nq)),
            dma((TICKS, nq)),
            dma((TICKS, nq)),
            dma((TICKS, nq)),
            dma((3, nq)),
            dma((3, nq)),
            dma((TICKS, nq)),
        ],
        compiler_params=pltpu.CompilerParams(
            collective_id=0, has_side_effects=True, vmem_limit_bytes=60 * 2**20
        ),
        cost_estimate=pl.CostEstimate(flops=flops, bytes_accessed=read, transcendentals=0),
    )(stream, w_query, w_out, neighbour_kv)


def copy_kernel(first_in, second_in, first_out, second_out, held, in_sem, out_sem):
    moves = []
    for i, (source, target) in enumerate(((first_in, first_out), (second_in, second_out))):
        rows = source.shape[0] // in_sem.shape[1]
        for j in range(in_sem.shape[1]):
            at = pl.ds(j * rows, rows)
            fetch = pltpu.make_async_copy(source.at[at], held.at[i, at], in_sem.at[i, j])
            store = pltpu.make_async_copy(held.at[i, at], target.at[at], out_sem.at[i, j])
            fetch.start()
            moves.append((fetch, store))
    for fetch, store in moves:
        fetch.wait()
        store.start()
    for fetch, store in moves:
        store.wait()


def copied(first, second):
    hbm = pl.BlockSpec(memory_space=pl.ANY)
    return pl.pallas_call(
        copy_kernel,
        out_shape=[jax.ShapeDtypeStruct(a.shape, a.dtype) for a in (first, second)],
        in_specs=[hbm] * 2,
        out_specs=[hbm] * 2,
        scratch_shapes=[
            pltpu.VMEM((2,) + first.shape, first.dtype),
            pltpu.SemaphoreType.DMA((2, 4)),
            pltpu.SemaphoreType.DMA((2, 4)),
        ],
        compiler_params=pltpu.CompilerParams(vmem_limit_bytes=60 * 2**20),
        cost_estimate=pl.CostEstimate(flops=0, bytes_accessed=8 * first.size, transcendentals=0),
    )(first, second)


def fits(stream, w_query, neighbour_kv):
    rows, width = stream.shape
    cols = w_query.shape[1]
    return (
        lax.axis_size("segment") == SECT
        and rows == 2 * CH
        and neighbour_kv.shape[2] == 2 * NEIGH * NBL
        and cols % (8 * HD) == 0
        and width % (cols // (2 * HD) * 128) == 0
        and cols // (2 * HD) == 2 * AHEAD
        and 2 * width * cols * 2 + neighbour_kv.size * 2 <= 42 * 2**20
    )


def per_device(stream, w_query, w_out, neighbour_kv):
    if fits(stream, w_query, neighbour_kv):
        return tuple(copied(*relay_call(stream, w_query, w_out, neighbour_kv)))
    groups_per = lax.axis_size("segment") // SECT
    head_group = lax.axis_index("segment") % groups_per
    total_bits = groups_per.bit_length() - 1
    bit_order = list(range(total_bits))
    edge_rows = NEIGH * NBL
    edges = passed_along(neighbour_kv[:, :, neighbour_kv.shape[2] - edge_rows :, :], "seq", 1)
    current = stream
    whole = assemble(current, head_group, bit_order, total_bits)
    outputs = []
    for tick_no in range(TICKS):
        term = local_layer(whole, neighbour_kv[tick_no], edges[tick_no], w_query, w_out)
        summed = share_sums(term, head_group, bit_order, total_bits)
        result = (current.astype(jnp.float32) + summed).astype(jnp.bfloat16)
        outputs.append(result)
        if tick_no + 1 < TICKS:
            current = passed_along(result, "segment", groups_per)
            whole = assemble(current, head_group, bit_order, total_bits)
    return (outputs[0], outputs[TICKS - 1])


def solution(mesh):
    placed = (
        P("seq", "segment"),
        P(None, "segment"),
        P("segment", None),
        P(None, None, "seq", "segment"),
    )
    return jax.shard_map(
        per_device,
        mesh=mesh,
        in_specs=placed,
        out_specs=(P("seq", "segment"), P("seq", "segment")),
        check_vma=False,
    )
```

```python
import jax
import jax.numpy as jnp
from jax import lax
from jax.experimental import pallas as pl
from jax.experimental.pallas import tpu as pltpu
from jax.sharding import PartitionSpec as P

HD = 128
SECT = 8
CH = 64
NEIGH = 2
NBL = 128
TICKS = 2


EPS = 1e-05


def swapped(block, axis, apart):
    count = lax.axis_size(axis)
    route = []
    for low in range(count):
        high = low | 1 << apart
        if high != low and high < count:
            route += [(low, high), (high, low)]
    return lax.ppermute(block, axis, route)


def passed_along(block, axis, distance):
    devices = range(lax.axis_size(axis))
    route = [(i - distance, i) for i in devices if i - distance in devices]
    return lax.ppermute(block, axis, route)


def assemble(piece, head_group, bit_order, total_bits):
    current = piece
    for bit_index in bit_order:
        other = swapped(current, "segment", bit_index)
        is_upper = head_group // 2**bit_index % 2 == 1
        lower_half = jnp.where(is_upper, other, current)
        upper_half = jnp.where(is_upper, current, other)
        current = jnp.stack([lower_half, upper_half], axis=1)
    count_bits = len(bit_order)
    permutation = [0]
    for target in range(count_bits):
        wanted = total_bits - 1 - target
        permutation.append(1 + (count_bits - 1 - bit_order.index(wanted)))
    permutation.append(count_bits + 1)
    if count_bits > 0:
        current = jnp.transpose(current, permutation)
    return current.reshape(piece.shape[0], -1)


def share_sums(term, head_group, bit_order, total_bits):
    partial_value = term.astype(jnp.float32)
    tok_rows = partial_value.shape[0]
    current = partial_value.reshape(
        (tok_rows,) + (2,) * total_bits + (partial_value.shape[1] // 2**total_bits,)
    )
    remaining = list(range(total_bits - 1, -1, -1))
    for bit_index in bit_order:
        axis_pos = 1 + remaining.index(bit_index)
        lower_half = lax.index_in_dim(current, 0, axis_pos, keepdims=False)
        upper_half = lax.index_in_dim(current, 1, axis_pos, keepdims=False)
        is_upper = head_group // 2**bit_index % 2 == 1
        kept_half = jnp.where(is_upper, upper_half, lower_half)
        sent_half = jnp.where(is_upper, lower_half, upper_half)
        current = kept_half + swapped(sent_half.astype(jnp.bfloat16), "segment", bit_index).astype(
            sent_half.dtype
        )
        remaining = [bit_left for bit_left in remaining if bit_left != bit_index]
    return current


def local_layer(whole, keys_values, edge_kv, w_query, w_out):
    wide = whole.astype(jnp.float32)
    normed = (wide * lax.rsqrt(jnp.mean(wide * wide, axis=-1, keepdims=True) + EPS)).astype(
        jnp.bfloat16
    )
    queries = jnp.dot(normed, w_query, preferred_element_type=jnp.float32).astype(jnp.bfloat16)
    tokens = queries.shape[0]
    head_cols = queries.shape[1]
    groups = tokens // CH + 1
    padded = jnp.concatenate(
        [
            jnp.zeros((1, head_cols), jnp.bfloat16),
            queries,
            jnp.zeros((CH - 1, head_cols), jnp.bfloat16),
        ],
        axis=0,
    )
    padded = padded.reshape(groups, CH, head_cols // HD, HD)
    extended = jnp.concatenate([edge_kv, keys_values], axis=1).reshape(
        2, groups, NEIGH * NBL, head_cols // HD, HD
    )
    scores = jnp.einsum(
        "gchd,gkhd->ghck", padded, extended[0], preferred_element_type=jnp.float32
    ) * HD ** (-0.5)
    exponent = jnp.exp(scores)
    weights = (exponent / jnp.sum(exponent, axis=-1, keepdims=True)).astype(jnp.bfloat16)
    attended = jnp.einsum(
        "ghck,gkhd->gchd", weights, extended[1], preferred_element_type=jnp.float32
    ).astype(jnp.bfloat16)
    attended = attended.reshape(-1, head_cols)[1 : 1 + tokens]
    term = jnp.dot(attended, w_out, preferred_element_type=jnp.float32).astype(jnp.bfloat16)
    return lax.optimization_barrier(term)


MESH = pl.DeviceIdType.MESH
LAG = 3
TAIL = 16
AHEAD = 2


def relay_kernel(
    x_hbm, wq_hbm, wo_hbm, kv_hbm, first_hbm, second_hbm,
    x_v, wq_v, wo_v, kv_v, x2_v, y_v, y2_v, acc_v, q_v, hq_v, ha_v, la_v, lb_v, att_v, r_v,
    x_sem, wq_sem, wo_sem, kv_sem, hq_send, hq_recv, ha_send, ha_recv,
    rel_send, rel_recv, out_sem,
):
    _, nq, _, cw = q_v.shape
    nf, fw = nq, x_v.shape[1] // nq
    halves, width, wide_cols = wq_v.shape
    quarters, cols, wide_features = wo_v.shape
    per_half, per_quarter = nq // halves, nf // quarters
    keys = kv_v.shape[2]
    half = keys // 2
    k, s = lax.axis_index("seq"), lax.axis_index("segment")
    nk, ns = lax.axis_size("seq"), lax.axis_size("segment")
    has_prev, has_next = k > 0, k < nk - 1
    has_in, has_out = s > 0, s < ns - 1
    prev = (lax.rem(k + nk - 1, nk), s)
    following = (lax.rem(k + 1, nk), s)
    below = (k, lax.rem(s + ns - 1, ns))
    above = (k, lax.rem(s + 1, ns))
    top, low = pl.ds(0, CH), pl.ds(CH, CH)
    last_row = lax.broadcasted_iota(jnp.int32, (CH, cw), 0) == CH - 1

    def head_cols(n):
        return pl.ds(pl.multiple_of(n * cw, cw), cw)

    def feature_cols(c):
        return pl.ds(pl.multiple_of(c * fw, fw), fw)

    def load_wq(h):
        source = wq_hbm.at[:, pl.ds(h * wide_cols, wide_cols)]
        return pltpu.make_async_copy(source, wq_v.at[h], wq_sem.at[h])

    def load_kv(t):
        return pltpu.make_async_copy(kv_hbm.at[t], kv_v.at[t], kv_sem.at[t])

    def load_wo(g):
        source = wo_hbm.at[:, pl.ds(g * wide_features, wide_features)]
        return pltpu.make_async_copy(source, wo_v.at[g], wo_sem.at[g])

    weights = [load_wq(h) for h in range(halves)] + [load_wo(g) for g in range(quarters)]

    def await_wq(h):
        load_wq(h).wait()
        weights[h + AHEAD].start()

    def halo_q(t, n):
        return pltpu.make_async_remote_copy(
            src_ref=q_v.at[t, n, top], dst_ref=hq_v.at[t, n],
            send_sem=hq_send, recv_sem=hq_recv.at[t, n],
            device_id=prev, device_id_type=MESH,
        )

    def halo_a(t, n):
        return pltpu.make_async_remote_copy(
            src_ref=ha_v.at[t, n], dst_ref=att_v.at[t, top, head_cols(n)],
            send_sem=ha_send, recv_sem=ha_recv.at[t, n],
            device_id=following, device_id_type=MESH,
        )

    parts = (pl.ds(0, CH), pl.ds(2 * CH - TAIL, TAIL), pl.ds(CH, CH - TAIL))

    def relay(b, g):
        rows, at = parts[b], pl.ds(pl.multiple_of(g * wide_features, wide_features), wide_features)
        return pltpu.make_async_remote_copy(
            src_ref=y_v.at[rows, at], dst_ref=x2_v.at[rows, at],
            send_sem=rel_send, recv_sem=rel_recv.at[b, g],
            device_id=above, device_id_type=MESH,
        )

    def store(t, g):
        buffer, target = ((y_v, first_hbm), (y2_v, second_hbm))[t]
        at = pl.ds(pl.multiple_of(g * wide_features, wide_features), wide_features)
        return pltpu.make_async_copy(buffer.at[:, at], target.at[:, at], out_sem.at[t])

    ones = jnp.ones((half, HD), jnp.bfloat16)

    def attend(block, t, n, span):
        at_keys = pl.ds(span * half, half)
        heads = []
        for h in range(cw // HD):
            at = pl.ds(pl.multiple_of(n * cw + h * HD, HD), HD)
            scores = lax.dot_general(
                block[:, h * HD:(h + 1) * HD], kv_v[t, 0, at_keys, at], (((1,), (1,)), ((), ())),
                preferred_element_type=jnp.float32,
            )
            most = jnp.max(scores, axis=1, keepdims=True)
            exponent = jnp.exp((scores - most) * HD ** (-0.5)).astype(jnp.bfloat16)
            values = jnp.concatenate([kv_v[t, 1, at_keys, at], ones], axis=1)
            both = jnp.dot(exponent, values, preferred_element_type=jnp.float32)
            heads.append(both[:, :HD] / both[:, HD:])
        return jnp.concatenate(heads, axis=1).astype(jnp.bfloat16)

    def loop(start, stop, body):
        def step(i, carry):
            body(i)
            return carry

        lax.fori_loop(start, stop, step, 0)

    load_x = pltpu.make_async_copy(x_hbm, x_v, x_sem)
    load_x.start()
    weights[0].start()
    load_kv(0).start()
    for i in range(1, AHEAD):
        weights[i].start()

    barrier = pltpu.get_barrier_semaphore()
    pairs = ((has_prev, prev), (has_next, following), (has_in, below), (has_out, above))
    for exists, device in pairs:

        @pl.when(exists)
        def _(device=device):
            pl.semaphore_signal(barrier, inc=1, device_id=device, device_id_type=MESH)

    @pl.when(jnp.logical_not(has_next))
    def _():
        hq_v[:, :nq] = jnp.zeros_like(hq_v[:, :nq])

    @pl.when(jnp.logical_not(has_prev))
    def _():
        att_v[:, top, :] = jnp.zeros_like(att_v[:, top, :])

    @pl.when(jnp.logical_not(has_in))
    def _():
        x2_v[...] = jnp.zeros_like(x2_v)

    acc_v[...] = jnp.zeros_like(acc_v)
    hq_v[0, nq] = jnp.zeros_like(hq_v[0, nq])
    load_x.wait()
    wide = x_v[...].astype(jnp.float32)
    scale = lax.rsqrt(jnp.mean(wide * wide, axis=1, keepdims=True) + EPS)
    r_v[...] = jnp.broadcast_to(scale, r_v.shape)
    pl.semaphore_wait(barrier, sum(exists.astype(jnp.int32) for exists, _ in pairs))

    def keep_own(t, n, out):
        at = head_cols(n)
        att_v[t, low, at] = out
        la_v[:, at] = out[CH - TAIL:]

    def join(t):
        @pl.when(has_prev)
        def _():
            loop(0, nq, lambda n: halo_a(t, n).wait_recv())

        end = lax.broadcasted_iota(jnp.int32, la_v.shape, 0) == TAIL - 1
        top_end, low_end = pl.ds(CH - TAIL, TAIL), pl.ds(2 * CH - TAIL, TAIL)
        att_v[t, top_end] = jnp.where(end, la_v[...], att_v[t, top_end])
        att_v[t, low_end] = jnp.where(end, lb_v[...], att_v[t, low_end])

    def step(c, with_q, with_attention):
        other = c - LAG
        ready = other >= 0
        own, n = jnp.minimum(c - 1, nq - 1), jnp.maximum(other, 0)
        slot = jnp.where(ready, other, nq)
        if with_q:
            for h in range(1, halves):

                @pl.when(c == h * per_half)
                def _():
                    await_wq(h)

        if with_attention:

            @pl.when(jnp.logical_and(ready, has_next))
            def _():
                halo_q(0, n).wait_recv()

            own_block = jnp.where(last_row, q_v[0, own, top], q_v[0, own, low])
            halo_block = jnp.where(last_row, q_v[0, n, low], hq_v[0, slot])
        if with_q:
            at = pl.ds(pl.multiple_of(c % per_half * cw, cw), cw)
            weight = wq_v[c // per_half, :, at]
            total = jnp.dot(x_v[...], weight, preferred_element_type=jnp.float32)
            made = (total * r_v[:, :1]).astype(jnp.bfloat16)
        if with_attention:
            own_out = attend(own_block, 0, own, 0)
            halo_out = attend(halo_block, 0, n, 1)
        if with_q:
            q_v[0, c] = made

            @pl.when(has_prev)
            def _():
                halo_q(0, c).start()

        if with_attention:
            ha_v[0, slot] = halo_out
            lb_v[:, head_cols(n)] = halo_out[CH - TAIL:]

            @pl.when(jnp.logical_and(ready, has_next))
            def _():
                halo_a(0, n).start()

            keep_own(0, own, own_out)

    await_wq(0)
    step(0, True, False)
    load_kv(0).wait()
    loop(1, nq, lambda c: step(c, True, True))
    for copy in weights[halves + AHEAD:]:
        copy.start()
    load_kv(1).start()
    loop(nq, nq + LAG, lambda c: step(c, False, True))
    join(0)

    def project(t, c):
        at = pl.ds(pl.multiple_of(c % per_quarter * fw, fw), fw)
        weight = wo_v[c // per_quarter, :, at]
        term = jnp.dot(att_v[t], weight, preferred_element_type=jnp.float32)
        return term.astype(jnp.bfloat16).astype(jnp.float32)

    def first_chunk(c):
        g, at = c // per_quarter, feature_cols(c)

        @pl.when(c % per_quarter == 0)
        def _():
            load_wo(g).wait()

        residual = x_v[:, at].astype(jnp.float32)
        y_v[:, at] = (residual + project(0, c)).astype(jnp.bfloat16)

        @pl.when(c % per_quarter == per_quarter - 1)
        def _():
            @pl.when(has_out)
            def _():
                relay(0, g).start()
                relay(1, g).start()

            store(0, g).start()

    loop(0, nf, first_chunk)

    @pl.when(has_out)
    def _():
        loop(0, quarters, lambda g: relay(2, g).start())

    def await_relay(c, which):
        @pl.when(jnp.logical_and(c % per_quarter == 0, has_in))
        def _():
            for b in which:
                relay(b, c // per_quarter).wait_recv()

    def gather_early(c):
        await_relay(c, (0, 1))
        at = feature_cols(c)
        block = jnp.concatenate([x2_v[parts[0], at], x2_v[parts[1], at]], axis=0)
        for h in range(halves):
            made = jnp.dot(block, wq_v[h, at, :], preferred_element_type=jnp.float32)
            acc_v[h, parts[0]] += made[:CH]
            acc_v[h, parts[1]] += made[CH:]

    loop(0, nf, gather_early)

    def scale_rows(rows):
        block = x2_v[rows].astype(jnp.float32)
        return lax.rsqrt(jnp.mean(block * block, axis=1, keepdims=True) + EPS)

    def make_queries(rows):
        scale = scale_rows(rows)
        for n in range(nq):
            at = pl.ds(n % per_half * cw, cw)
            q_v[1, n, rows] = (acc_v[n // per_half, rows, at] * scale).astype(jnp.bfloat16)

    for rows in parts[:2]:
        make_queries(rows)

    @pl.when(has_prev)
    def _():
        loop(0, nq, lambda n: halo_q(1, n).start())

    def gather_late(c):
        await_relay(c, (2,))
        at = feature_cols(c)
        block = x2_v[parts[2], at]
        for h in range(halves):
            acc_v[h, parts[2]] += jnp.dot(
                block, wq_v[h, at, :], preferred_element_type=jnp.float32
            )

    loop(0, nf, gather_late)
    make_queries(parts[2])
    load_kv(1).wait()

    def finish(n):
        @pl.when(has_next)
        def _():
            halo_q(1, n).wait_recv()

        block = q_v[1, n, low]
        halo_block = jnp.where(last_row, block, hq_v[1, n])
        own_block = jnp.where(last_row, q_v[1, n, top], block)
        halo_out = attend(halo_block, 1, n, 1)
        own_out = attend(own_block, 1, n, 0)
        ha_v[1, n] = halo_out
        lb_v[:, head_cols(n)] = halo_out[CH - TAIL:]

        @pl.when(has_next)
        def _():
            halo_a(1, n).start()

        keep_own(1, n, own_out)

    loop(0, nq, finish)
    join(1)

    def second_chunk(c):
        at = feature_cols(c)
        y2_v[:, at] = (x2_v[:, at].astype(jnp.float32) + project(1, c)).astype(jnp.bfloat16)

        @pl.when(c % per_quarter == per_quarter - 1)
        def _():
            store(1, c // per_quarter).start()

    loop(0, nf, second_chunk)

    halo = ha_v.at[:, pl.ds(0, nq)]

    @pl.when(has_prev)
    def _():
        pltpu.make_async_remote_copy(
            src_ref=halo, dst_ref=halo, send_sem=hq_send, recv_sem=hq_send,
            device_id=prev, device_id_type=MESH,
        ).wait_send()

    @pl.when(has_next)
    def _():
        pltpu.make_async_remote_copy(
            src_ref=halo, dst_ref=halo, send_sem=ha_send, recv_sem=ha_send,
            device_id=following, device_id_type=MESH,
        ).wait_send()

    @pl.when(has_out)
    def _():
        pltpu.make_async_remote_copy(
            src_ref=y_v, dst_ref=x2_v, send_sem=rel_send, recv_sem=rel_send,
            device_id=above, device_id_type=MESH,
        ).wait_send()

    pltpu.make_async_copy(y_v, first_hbm, out_sem.at[0]).wait()
    pltpu.make_async_copy(y2_v, second_hbm, out_sem.at[1]).wait()


def relay_call(stream, w_query, w_out, neighbour_kv):
    rows, width = stream.shape
    cols = w_query.shape[1]
    keys = neighbour_kv.shape[2]
    cw = 2 * HD
    nq = cols // cw
    bf16, dma = jnp.bfloat16, pltpu.SemaphoreType.DMA
    hbm = pl.BlockSpec(memory_space=pl.ANY)
    flops = TICKS * 2 * rows * cols * (2 * width + 4 * keys)
    read = 2 * (stream.size + w_query.size + w_out.size + neighbour_kv.size + 2 * stream.size)
    return pl.pallas_call(
        relay_kernel,
        out_shape=[jax.ShapeDtypeStruct(stream.shape, bf16)] * 2,
        in_specs=[hbm] * 4,
        out_specs=[hbm] * 2,
        scratch_shapes=[
            pltpu.VMEM((rows, width), bf16),
            pltpu.VMEM((4, width, cols // 4), bf16),
            pltpu.VMEM((4, cols, width // 4), bf16),
            pltpu.VMEM((TICKS, 2, keys, cols), bf16),
            pltpu.VMEM((rows, width), bf16),
            pltpu.VMEM((rows, width), bf16),
            pltpu.VMEM((rows, width), bf16),
            pltpu.VMEM((4, rows, cols // 4), jnp.float32),
            pltpu.VMEM((TICKS, nq, rows, cw), bf16),
            pltpu.VMEM((TICKS, nq + 1, CH, cw), bf16),
            pltpu.VMEM((TICKS, nq + 1, CH, cw), bf16),
            pltpu.VMEM((TAIL, cols), bf16),
            pltpu.VMEM((TAIL, cols), bf16),
            pltpu.VMEM((TICKS, rows, cols), bf16),
            pltpu.VMEM((rows, 128), jnp.float32),
            dma,
            dma((4,)),
            dma((4,)),
            dma((TICKS,)),
            dma,
            dma((TICKS, nq)),
            dma,
            dma((TICKS, nq)),
            dma,
            dma((3, 4)),
            dma((TICKS,)),
        ],
        compiler_params=pltpu.CompilerParams(
            collective_id=0, has_side_effects=True, vmem_limit_bytes=60 * 2**20
        ),
        cost_estimate=pl.CostEstimate(flops=flops, bytes_accessed=read, transcendentals=0),
    )(stream, w_query, w_out, neighbour_kv)


def copy_kernel(first_in, second_in, first_out, second_out, held, in_sem, out_sem):
    moves = []
    for i, (source, target) in enumerate(((first_in, first_out), (second_in, second_out))):
        rows = source.shape[0] // in_sem.shape[1]
        for j in range(in_sem.shape[1]):
            at = pl.ds(j * rows, rows)
            fetch = pltpu.make_async_copy(source.at[at], held.at[i, at], in_sem.at[i, j])
            store = pltpu.make_async_copy(held.at[i, at], target.at[at], out_sem.at[i, j])
            fetch.start()
            moves.append((fetch, store))
    for fetch, store in moves:
        fetch.wait()
        store.start()
    for fetch, store in moves:
        store.wait()


def copied(first, second):
    hbm = pl.BlockSpec(memory_space=pl.ANY)
    return pl.pallas_call(
        copy_kernel,
        out_shape=[jax.ShapeDtypeStruct(a.shape, a.dtype) for a in (first, second)],
        in_specs=[hbm] * 2,
        out_specs=[hbm] * 2,
        scratch_shapes=[
            pltpu.VMEM((2,) + first.shape, first.dtype),
            pltpu.SemaphoreType.DMA((2, 4)),
            pltpu.SemaphoreType.DMA((2, 4)),
        ],
        compiler_params=pltpu.CompilerParams(vmem_limit_bytes=60 * 2**20),
        cost_estimate=pl.CostEstimate(flops=0, bytes_accessed=8 * first.size, transcendentals=0),
    )(first, second)


def fits(stream, w_query, neighbour_kv):
    rows, width = stream.shape
    cols = w_query.shape[1]
    return (
        lax.axis_size("segment") == SECT
        and rows == 2 * CH
        and neighbour_kv.shape[2] == 2 * NEIGH * NBL
        and cols % (8 * HD) == 0
        and width % (cols // (2 * HD) * 128) == 0
        and cols // (2 * HD) == 8
        and 2 * width * cols * 2 + neighbour_kv.size * 2 <= 42 * 2**20
    )


def per_device(stream, w_query, w_out, neighbour_kv):
    if fits(stream, w_query, neighbour_kv):
        return tuple(copied(*relay_call(stream, w_query, w_out, neighbour_kv)))
    groups_per = lax.axis_size("segment") // SECT
    head_group = lax.axis_index("segment") % groups_per
    total_bits = groups_per.bit_length() - 1
    bit_order = list(range(total_bits))
    edge_rows = NEIGH * NBL
    edges = passed_along(neighbour_kv[:, :, neighbour_kv.shape[2] - edge_rows :, :], "seq", 1)
    current = stream
    whole = assemble(current, head_group, bit_order, total_bits)
    outputs = []
    for tick_no in range(TICKS):
        term = local_layer(whole, neighbour_kv[tick_no], edges[tick_no], w_query, w_out)
        summed = share_sums(term, head_group, bit_order, total_bits)
        result = (current.astype(jnp.float32) + summed).astype(jnp.bfloat16)
        outputs.append(result)
        if tick_no + 1 < TICKS:
            current = passed_along(result, "segment", groups_per)
            whole = assemble(current, head_group, bit_order, total_bits)
    return (outputs[0], outputs[TICKS - 1])


def solution(mesh):
    placed = (
        P("seq", "segment"),
        P(None, "segment"),
        P("segment", None),
        P(None, None, "seq", "segment"),
    )
    return jax.shard_map(
        per_device,
        mesh=mesh,
        in_specs=placed,
        out_specs=(P("seq", "segment"), P("seq", "segment")),
        check_vma=False,
    )
```

```python
import jax
import jax.numpy as jnp
from jax import lax
from jax.experimental import pallas as pl
from jax.experimental.pallas import tpu as pltpu
from jax.sharding import PartitionSpec as P

HD = 128
SECT = 8
CH = 64
NEIGH = 2
NBL = 128
TICKS = 2


EPS = 1e-05


def swapped(block, axis, apart):
    count = lax.axis_size(axis)
    route = []
    for low in range(count):
        high = low | 1 << apart
        if high != low and high < count:
            route += [(low, high), (high, low)]
    return lax.ppermute(block, axis, route)


def passed_along(block, axis, distance):
    devices = range(lax.axis_size(axis))
    route = [(i - distance, i) for i in devices if i - distance in devices]
    return lax.ppermute(block, axis, route)


def assemble(piece, head_group, bit_order, total_bits):
    current = piece
    for bit_index in bit_order:
        other = swapped(current, "segment", bit_index)
        is_upper = head_group // 2**bit_index % 2 == 1
        lower_half = jnp.where(is_upper, other, current)
        upper_half = jnp.where(is_upper, current, other)
        current = jnp.stack([lower_half, upper_half], axis=1)
    count_bits = len(bit_order)
    permutation = [0]
    for target in range(count_bits):
        wanted = total_bits - 1 - target
        permutation.append(1 + (count_bits - 1 - bit_order.index(wanted)))
    permutation.append(count_bits + 1)
    if count_bits > 0:
        current = jnp.transpose(current, permutation)
    return current.reshape(piece.shape[0], -1)


def share_sums(term, head_group, bit_order, total_bits):
    partial_value = term.astype(jnp.float32)
    tok_rows = partial_value.shape[0]
    current = partial_value.reshape(
        (tok_rows,) + (2,) * total_bits + (partial_value.shape[1] // 2**total_bits,)
    )
    remaining = list(range(total_bits - 1, -1, -1))
    for bit_index in bit_order:
        axis_pos = 1 + remaining.index(bit_index)
        lower_half = lax.index_in_dim(current, 0, axis_pos, keepdims=False)
        upper_half = lax.index_in_dim(current, 1, axis_pos, keepdims=False)
        is_upper = head_group // 2**bit_index % 2 == 1
        kept_half = jnp.where(is_upper, upper_half, lower_half)
        sent_half = jnp.where(is_upper, lower_half, upper_half)
        current = kept_half + swapped(sent_half.astype(jnp.bfloat16), "segment", bit_index).astype(
            sent_half.dtype
        )
        remaining = [bit_left for bit_left in remaining if bit_left != bit_index]
    return current


def local_layer(whole, keys_values, edge_kv, w_query, w_out):
    wide = whole.astype(jnp.float32)
    normed = (wide * lax.rsqrt(jnp.mean(wide * wide, axis=-1, keepdims=True) + EPS)).astype(
        jnp.bfloat16
    )
    queries = jnp.dot(normed, w_query, preferred_element_type=jnp.float32).astype(jnp.bfloat16)
    tokens = queries.shape[0]
    head_cols = queries.shape[1]
    groups = tokens // CH + 1
    padded = jnp.concatenate(
        [
            jnp.zeros((1, head_cols), jnp.bfloat16),
            queries,
            jnp.zeros((CH - 1, head_cols), jnp.bfloat16),
        ],
        axis=0,
    )
    padded = padded.reshape(groups, CH, head_cols // HD, HD)
    extended = jnp.concatenate([edge_kv, keys_values], axis=1).reshape(
        2, groups, NEIGH * NBL, head_cols // HD, HD
    )
    scores = jnp.einsum(
        "gchd,gkhd->ghck", padded, extended[0], preferred_element_type=jnp.float32
    ) * HD ** (-0.5)
    exponent = jnp.exp(scores)
    weights = (exponent / jnp.sum(exponent, axis=-1, keepdims=True)).astype(jnp.bfloat16)
    attended = jnp.einsum(
        "ghck,gkhd->gchd", weights, extended[1], preferred_element_type=jnp.float32
    ).astype(jnp.bfloat16)
    attended = attended.reshape(-1, head_cols)[1 : 1 + tokens]
    term = jnp.dot(attended, w_out, preferred_element_type=jnp.float32).astype(jnp.bfloat16)
    return lax.optimization_barrier(term)


MESH = pl.DeviceIdType.MESH
BASE = HD ** (-0.5) * 1.4426950408889634
LAG = 2
TAIL = 16
AHEAD = 2


def relay_kernel(
    x_hbm, wq_hbm, wo_hbm, kv_hbm, first_hbm, second_hbm,
    x_v, wq_v, wo_v, kv_v, x2_v, y_v, y2_v, acc_v, q_v, hq_v, ha_v, la_v, lb_v, att_v, r_v,
    x_sem, wq_sem, wo_sem, kv_sem, hq_send, hq_recv, ha_send, ha_recv,
    rel_send, rel_recv, out_sem,
):
    _, nq, _, cw = q_v.shape
    halves, width, wide_cols = wq_v.shape
    quarters, cols, wide_features = wo_v.shape
    per_half = nq // halves
    keys = kv_v.shape[2]
    half = keys // 2
    k, s = lax.axis_index("seq"), lax.axis_index("segment")
    nk, ns = lax.axis_size("seq"), lax.axis_size("segment")
    has_prev, has_next = k > 0, k < nk - 1
    has_in, has_out = s > 0, s < ns - 1
    prev = (lax.rem(k + nk - 1, nk), s)
    following = (lax.rem(k + 1, nk), s)
    below = (k, lax.rem(s + ns - 1, ns))
    above = (k, lax.rem(s + 1, ns))
    top, low = pl.ds(0, CH), pl.ds(CH, CH)
    last_row = lax.broadcasted_iota(jnp.int32, (CH, cw), 0) == CH - 1

    def head_cols(n):
        return pl.ds(pl.multiple_of(n * cw, cw), cw)

    def feature_cols(g):
        return pl.ds(pl.multiple_of(g * wide_features, wide_features), wide_features)

    def load_wq(h):
        source = wq_hbm.at[:, pl.ds(h * wide_cols, wide_cols)]
        return pltpu.make_async_copy(source, wq_v.at[h], wq_sem.at[h])

    def load_kv(t):
        return pltpu.make_async_copy(kv_hbm.at[t], kv_v.at[t], kv_sem.at[t])

    def load_wo(g):
        source = wo_hbm.at[:, pl.ds(g * wide_features, wide_features)]
        return pltpu.make_async_copy(source, wo_v.at[g], wo_sem.at[g])

    weights = [load_wq(h) for h in range(halves)] + [load_wo(g) for g in range(quarters)]

    def await_wq(h):
        load_wq(h).wait()
        weights[h + AHEAD].start()

    def halo_q(t, n):
        return pltpu.make_async_remote_copy(
            src_ref=q_v.at[t, n, top], dst_ref=hq_v.at[t, n],
            send_sem=hq_send, recv_sem=hq_recv.at[t, n],
            device_id=prev, device_id_type=MESH,
        )

    def halo_a(t, n):
        return pltpu.make_async_remote_copy(
            src_ref=ha_v.at[t, n], dst_ref=att_v.at[t, top, head_cols(n)],
            send_sem=ha_send, recv_sem=ha_recv.at[t, n],
            device_id=following, device_id_type=MESH,
        )

    parts = (pl.ds(0, CH), pl.ds(2 * CH - TAIL, TAIL), pl.ds(CH, CH - TAIL))

    def relay(b, g):
        rows, at = parts[b], pl.ds(pl.multiple_of(g * wide_features, wide_features), wide_features)
        return pltpu.make_async_remote_copy(
            src_ref=y_v.at[rows, at], dst_ref=x2_v.at[rows, at],
            send_sem=rel_send, recv_sem=rel_recv.at[b, g],
            device_id=above, device_id_type=MESH,
        )

    def store(t, g):
        buffer, target = ((y_v, first_hbm), (y2_v, second_hbm))[t]
        at = pl.ds(pl.multiple_of(g * wide_features, wide_features), wide_features)
        return pltpu.make_async_copy(buffer.at[:, at], target.at[:, at], out_sem.at[t])

    ones = jnp.ones((half, HD), jnp.bfloat16)

    def attend(block, t, n, span):
        at_keys = pl.ds(span * half, half)
        heads = []
        for h in range(cw // HD):
            at = pl.ds(pl.multiple_of(n * cw + h * HD, HD), HD)
            scores = lax.dot_general(
                block[:, h * HD:(h + 1) * HD], kv_v[t, 0, at_keys, at], (((1,), (1,)), ((), ())),
                preferred_element_type=jnp.float32,
            )
            most = jnp.max(scores, axis=1, keepdims=True)
            exponent = jnp.exp2((scores - most) * BASE).astype(jnp.bfloat16)
            values = jnp.concatenate([kv_v[t, 1, at_keys, at], ones], axis=1)
            both = jnp.dot(exponent, values, preferred_element_type=jnp.float32)
            heads.append(both[:, :HD] / both[:, HD:])
        return jnp.concatenate(heads, axis=1).astype(jnp.bfloat16)

    def loop(start, stop, body):
        def step(i, carry):
            body(i)
            return carry

        lax.fori_loop(start, stop, step, 0)

    load_x = pltpu.make_async_copy(x_hbm, x_v, x_sem)
    load_x.start()
    weights[0].start()

    barrier = pltpu.get_barrier_semaphore()
    pairs = ((has_prev, prev), (has_next, following), (has_in, below), (has_out, above))
    for exists, device in pairs:

        @pl.when(exists)
        def _(device=device):
            pl.semaphore_signal(barrier, inc=1, device_id=device, device_id_type=MESH)

    @pl.when(jnp.logical_not(has_next))
    def _():
        hq_v[...] = jnp.zeros_like(hq_v)

    @pl.when(jnp.logical_not(has_prev))
    def _():
        att_v[:, top, :] = jnp.zeros_like(att_v[:, top, :])

    @pl.when(jnp.logical_not(has_in))
    def _():
        x2_v[...] = jnp.zeros_like(x2_v)

    acc_v[...] = jnp.zeros_like(acc_v)
    load_x.wait()
    load_kv(0).start()
    weights[1].start()
    wide = x_v[...].astype(jnp.float32)
    scale = lax.rsqrt(jnp.mean(wide * wide, axis=1, keepdims=True) + EPS)
    r_v[...] = jnp.broadcast_to(scale, r_v.shape)
    pl.semaphore_wait(barrier, sum(exists.astype(jnp.int32) for exists, _ in pairs))

    def keep_own(t, n, out):
        at = head_cols(n)
        att_v[t, low, at] = out
        la_v[:, at] = out[CH - TAIL:]

    def join(t):
        @pl.when(has_prev)
        def _():
            loop(0, nq, lambda n: halo_a(t, n).wait_recv())

        end = lax.broadcasted_iota(jnp.int32, la_v.shape, 0) == TAIL - 1
        top_end, low_end = pl.ds(CH - TAIL, TAIL), pl.ds(2 * CH - TAIL, TAIL)
        att_v[t, top_end] = jnp.where(end, la_v[...], att_v[t, top_end])
        att_v[t, low_end] = jnp.where(end, lb_v[...], att_v[t, low_end])

    def step(c, with_q, with_attention):
        n = c - LAG
        if with_q:
            for h in range(1, halves):

                @pl.when(c == h * per_half)
                def _():
                    await_wq(h)

            at = pl.ds(pl.multiple_of(c % per_half * cw, cw), cw)
        if with_attention:

            @pl.when(has_next)
            def _():
                halo_q(0, n).wait_recv()

            block = q_v[0, n, low]
            own_block = jnp.where(last_row, q_v[0, n, top], block)
            halo_block = jnp.where(last_row, block, hq_v[0, n])
        if with_q:
            weight = wq_v[c // per_half, :, at]
            total = jnp.dot(x_v[...], weight, preferred_element_type=jnp.float32)
            made = (total * r_v[:, :1]).astype(jnp.bfloat16)
        if with_attention:
            halo_out = attend(halo_block, 0, n, 1)
            own_out = attend(own_block, 0, n, 0)
        if with_q:
            q_v[0, c] = made

            @pl.when(has_prev)
            def _():
                halo_q(0, c).start()

        if with_attention:
            ha_v[0, n] = halo_out

            @pl.when(has_next)
            def _():
                halo_a(0, n).start()

            lb_v[:, head_cols(n)] = halo_out[CH - TAIL:]
            keep_own(0, n, own_out)

    await_wq(0)
    loop(0, LAG, lambda c: step(c, True, False))
    load_kv(0).wait()
    loop(LAG, nq, lambda c: step(c, True, True))
    for copy in weights[halves + AHEAD:]:
        copy.start()
    load_kv(1).start()
    loop(nq, nq + LAG, lambda c: step(c, False, True))
    join(0)

    def project(t, g):
        term = jnp.dot(att_v[t], wo_v[g], preferred_element_type=jnp.float32)
        return term.astype(jnp.bfloat16).astype(jnp.float32)

    def first_chunk(g):
        load_wo(g).wait()
        at = feature_cols(g)
        residual = x_v[:, at].astype(jnp.float32)
        y_v[:, at] = (residual + project(0, g)).astype(jnp.bfloat16)

        @pl.when(has_out)
        def _():
            relay(0, g).start()
            relay(1, g).start()

        store(0, g).start()

    loop(0, quarters, first_chunk)

    @pl.when(has_out)
    def _():
        loop(0, quarters, lambda g: relay(2, g).start())

    def await_relay(g, which):
        @pl.when(has_in)
        def _():
            for b in which:
                relay(b, g).wait_recv()

    def gather_early(c):
        await_relay(c, (0, 1))
        at = feature_cols(c)
        block = jnp.concatenate([x2_v[parts[0], at], x2_v[parts[1], at]], axis=0)
        for h in range(halves):
            made = jnp.dot(block, wq_v[h, at, :], preferred_element_type=jnp.float32)
            acc_v[h, parts[0]] += made[:CH]
            acc_v[h, parts[1]] += made[CH:]

    loop(0, quarters, gather_early)

    def scale_rows(rows):
        block = x2_v[rows].astype(jnp.float32)
        return lax.rsqrt(jnp.mean(block * block, axis=1, keepdims=True) + EPS)

    def make_queries(rows):
        scale = scale_rows(rows)
        for n in range(nq):
            at = pl.ds(n % per_half * cw, cw)
            q_v[1, n, rows] = (acc_v[n // per_half, rows, at] * scale).astype(jnp.bfloat16)

    for rows in parts[:2]:
        make_queries(rows)

    @pl.when(has_prev)
    def _():
        loop(0, nq, lambda n: halo_q(1, n).start())

    def gather_late(c):
        await_relay(c, (2,))
        at = feature_cols(c)
        block = x2_v[parts[2], at]
        for h in range(halves):
            acc_v[h, parts[2]] += jnp.dot(
                block, wq_v[h, at, :], preferred_element_type=jnp.float32
            )

    loop(0, quarters, gather_late)
    make_queries(parts[2])
    load_kv(1).wait()

    def finish(pair):
        outs = []
        for n in (2 * pair, 2 * pair + 1):

            @pl.when(has_next)
            def _():
                halo_q(1, n).wait_recv()

        for n in (2 * pair, 2 * pair + 1):
            block = q_v[1, n, low]
            halo_block = jnp.where(last_row, block, hq_v[1, n])
            own_block = jnp.where(last_row, q_v[1, n, top], block)
            outs.append((n, attend(halo_block, 1, n, 1), attend(own_block, 1, n, 0)))
        for n, halo_out, _ in outs:
            ha_v[1, n] = halo_out

            @pl.when(has_next)
            def _():
                halo_a(1, n).start()

        for n, halo_out, own_out in outs:
            lb_v[:, head_cols(n)] = halo_out[CH - TAIL:]
            keep_own(1, n, own_out)

    loop(0, nq // 2, finish)
    join(1)

    def second_chunk(g):
        at = feature_cols(g)
        y2_v[:, at] = (x2_v[:, at].astype(jnp.float32) + project(1, g)).astype(jnp.bfloat16)
        store(1, g).start()

    loop(0, quarters, second_chunk)

    @pl.when(has_prev)
    def _():
        pltpu.make_async_remote_copy(
            src_ref=ha_v, dst_ref=ha_v, send_sem=hq_send, recv_sem=hq_send,
            device_id=prev, device_id_type=MESH,
        ).wait_send()

    @pl.when(has_next)
    def _():
        pltpu.make_async_remote_copy(
            src_ref=ha_v, dst_ref=ha_v, send_sem=ha_send, recv_sem=ha_send,
            device_id=following, device_id_type=MESH,
        ).wait_send()

    @pl.when(has_out)
    def _():
        pltpu.make_async_remote_copy(
            src_ref=y_v, dst_ref=x2_v, send_sem=rel_send, recv_sem=rel_send,
            device_id=above, device_id_type=MESH,
        ).wait_send()

    pltpu.make_async_copy(y_v, first_hbm, out_sem.at[0]).wait()
    pltpu.make_async_copy(y2_v, second_hbm, out_sem.at[1]).wait()


def relay_call(stream, w_query, w_out, neighbour_kv):
    rows, width = stream.shape
    cols = w_query.shape[1]
    keys = neighbour_kv.shape[2]
    cw = 2 * HD
    nq = cols // cw
    bf16, dma = jnp.bfloat16, pltpu.SemaphoreType.DMA
    hbm = pl.BlockSpec(memory_space=pl.ANY)
    flops = TICKS * 2 * rows * cols * (2 * width + 4 * keys)
    read = 2 * (stream.size + w_query.size + w_out.size + neighbour_kv.size + 2 * stream.size)
    return pl.pallas_call(
        relay_kernel,
        out_shape=[jax.ShapeDtypeStruct(stream.shape, bf16)] * 2,
        in_specs=[hbm] * 4,
        out_specs=[hbm] * 2,
        scratch_shapes=[
            pltpu.VMEM((rows, width), bf16),
            pltpu.VMEM((4, width, cols // 4), bf16),
            pltpu.VMEM((4, cols, width // 4), bf16),
            pltpu.VMEM((TICKS, 2, keys, cols), bf16),
            pltpu.VMEM((rows, width), bf16),
            pltpu.VMEM((rows, width), bf16),
            pltpu.VMEM((rows, width), bf16),
            pltpu.VMEM((4, rows, cols // 4), jnp.float32),
            pltpu.VMEM((TICKS, nq, rows, cw), bf16),
            pltpu.VMEM((TICKS, nq, CH, cw), bf16),
            pltpu.VMEM((TICKS, nq, CH, cw), bf16),
            pltpu.VMEM((TAIL, cols), bf16),
            pltpu.VMEM((TAIL, cols), bf16),
            pltpu.VMEM((TICKS, rows, cols), bf16),
            pltpu.VMEM((rows, 128), jnp.float32),
            dma,
            dma((4,)),
            dma((4,)),
            dma((TICKS,)),
            dma,
            dma((TICKS, nq)),
            dma,
            dma((TICKS, nq)),
            dma,
            dma((3, 4)),
            dma((TICKS,)),
        ],
        compiler_params=pltpu.CompilerParams(
            collective_id=0, has_side_effects=True, vmem_limit_bytes=60 * 2**20
        ),
        cost_estimate=pl.CostEstimate(flops=flops, bytes_accessed=read, transcendentals=0),
    )(stream, w_query, w_out, neighbour_kv)


def copy_kernel(first_in, second_in, first_out, second_out, held, in_sem, out_sem):
    moves = []
    for i, (source, target) in enumerate(((first_in, first_out), (second_in, second_out))):
        rows = source.shape[0] // in_sem.shape[1]
        for j in range(in_sem.shape[1]):
            at = pl.ds(j * rows, rows)
            fetch = pltpu.make_async_copy(source.at[at], held.at[i, at], in_sem.at[i, j])
            store = pltpu.make_async_copy(held.at[i, at], target.at[at], out_sem.at[i, j])
            fetch.start()
            moves.append((fetch, store))
    for fetch, store in moves:
        fetch.wait()
        store.start()
    for fetch, store in moves:
        store.wait()


def copied(first, second):
    hbm = pl.BlockSpec(memory_space=pl.ANY)
    return pl.pallas_call(
        copy_kernel,
        out_shape=[jax.ShapeDtypeStruct(a.shape, a.dtype) for a in (first, second)],
        in_specs=[hbm] * 2,
        out_specs=[hbm] * 2,
        scratch_shapes=[
            pltpu.VMEM((2,) + first.shape, first.dtype),
            pltpu.SemaphoreType.DMA((2, 4)),
            pltpu.SemaphoreType.DMA((2, 4)),
        ],
        compiler_params=pltpu.CompilerParams(vmem_limit_bytes=60 * 2**20),
        cost_estimate=pl.CostEstimate(flops=0, bytes_accessed=8 * first.size, transcendentals=0),
    )(first, second)


def fits(stream, w_query, neighbour_kv):
    rows, width = stream.shape
    cols = w_query.shape[1]
    return (
        lax.axis_size("segment") == SECT
        and rows == 2 * CH
        and neighbour_kv.shape[2] == 2 * NEIGH * NBL
        and cols % (8 * HD) == 0
        and width % (cols // (2 * HD) * 128) == 0
        and cols // (2 * HD) == 8
        and 2 * width * cols * 2 + neighbour_kv.size * 2 <= 42 * 2**20
    )


def per_device(stream, w_query, w_out, neighbour_kv):
    if fits(stream, w_query, neighbour_kv):
        return tuple(copied(*relay_call(stream, w_query, w_out, neighbour_kv)))
    groups_per = lax.axis_size("segment") // SECT
    head_group = lax.axis_index("segment") % groups_per
    total_bits = groups_per.bit_length() - 1
    bit_order = list(range(total_bits))
    edge_rows = NEIGH * NBL
    edges = passed_along(neighbour_kv[:, :, neighbour_kv.shape[2] - edge_rows :, :], "seq", 1)
    current = stream
    whole = assemble(current, head_group, bit_order, total_bits)
    outputs = []
    for tick_no in range(TICKS):
        term = local_layer(whole, neighbour_kv[tick_no], edges[tick_no], w_query, w_out)
        summed = share_sums(term, head_group, bit_order, total_bits)
        result = (current.astype(jnp.float32) + summed).astype(jnp.bfloat16)
        outputs.append(result)
        if tick_no + 1 < TICKS:
            current = passed_along(result, "segment", groups_per)
            whole = assemble(current, head_group, bit_order, total_bits)
    return (outputs[0], outputs[TICKS - 1])


def solution(mesh):
    placed = (
        P("seq", "segment"),
        P(None, "segment"),
        P("segment", None),
        P(None, None, "seq", "segment"),
    )
    return jax.shard_map(
        per_device,
        mesh=mesh,
        in_specs=placed,
        out_specs=(P("seq", "segment"), P("seq", "segment")),
        check_vma=False,
    )
```

```python
import jax
import jax.numpy as jnp
from jax import lax
from jax.experimental import pallas as pl
from jax.experimental.pallas import tpu as pltpu
from jax.sharding import PartitionSpec as P

HD = 128
SECT = 8
CH = 64
NEIGH = 2
NBL = 128
TICKS = 2


EPS = 1e-05


def swapped(block, axis, apart):
    count = lax.axis_size(axis)
    route = []
    for low in range(count):
        high = low | 1 << apart
        if high != low and high < count:
            route += [(low, high), (high, low)]
    return lax.ppermute(block, axis, route)


def passed_along(block, axis, distance):
    devices = range(lax.axis_size(axis))
    route = [(i - distance, i) for i in devices if i - distance in devices]
    return lax.ppermute(block, axis, route)


def assemble(piece, head_group, bit_order, total_bits):
    current = piece
    for bit_index in bit_order:
        other = swapped(current, "segment", bit_index)
        is_upper = head_group // 2**bit_index % 2 == 1
        lower_half = jnp.where(is_upper, other, current)
        upper_half = jnp.where(is_upper, current, other)
        current = jnp.stack([lower_half, upper_half], axis=1)
    count_bits = len(bit_order)
    permutation = [0]
    for target in range(count_bits):
        wanted = total_bits - 1 - target
        permutation.append(1 + (count_bits - 1 - bit_order.index(wanted)))
    permutation.append(count_bits + 1)
    if count_bits > 0:
        current = jnp.transpose(current, permutation)
    return current.reshape(piece.shape[0], -1)


def share_sums(term, head_group, bit_order, total_bits):
    partial_value = term.astype(jnp.float32)
    tok_rows = partial_value.shape[0]
    current = partial_value.reshape(
        (tok_rows,) + (2,) * total_bits + (partial_value.shape[1] // 2**total_bits,)
    )
    remaining = list(range(total_bits - 1, -1, -1))
    for bit_index in bit_order:
        axis_pos = 1 + remaining.index(bit_index)
        lower_half = lax.index_in_dim(current, 0, axis_pos, keepdims=False)
        upper_half = lax.index_in_dim(current, 1, axis_pos, keepdims=False)
        is_upper = head_group // 2**bit_index % 2 == 1
        kept_half = jnp.where(is_upper, upper_half, lower_half)
        sent_half = jnp.where(is_upper, lower_half, upper_half)
        current = kept_half + swapped(sent_half.astype(jnp.bfloat16), "segment", bit_index).astype(
            sent_half.dtype
        )
        remaining = [bit_left for bit_left in remaining if bit_left != bit_index]
    return current


def local_layer(whole, keys_values, edge_kv, w_query, w_out):
    wide = whole.astype(jnp.float32)
    normed = (wide * lax.rsqrt(jnp.mean(wide * wide, axis=-1, keepdims=True) + EPS)).astype(
        jnp.bfloat16
    )
    queries = jnp.dot(normed, w_query, preferred_element_type=jnp.float32).astype(jnp.bfloat16)
    tokens = queries.shape[0]
    head_cols = queries.shape[1]
    groups = tokens // CH + 1
    padded = jnp.concatenate(
        [
            jnp.zeros((1, head_cols), jnp.bfloat16),
            queries,
            jnp.zeros((CH - 1, head_cols), jnp.bfloat16),
        ],
        axis=0,
    )
    padded = padded.reshape(groups, CH, head_cols // HD, HD)
    extended = jnp.concatenate([edge_kv, keys_values], axis=1).reshape(
        2, groups, NEIGH * NBL, head_cols // HD, HD
    )
    scores = jnp.einsum(
        "gchd,gkhd->ghck", padded, extended[0], preferred_element_type=jnp.float32
    ) * HD ** (-0.5)
    exponent = jnp.exp(scores)
    weights = (exponent / jnp.sum(exponent, axis=-1, keepdims=True)).astype(jnp.bfloat16)
    attended = jnp.einsum(
        "ghck,gkhd->gchd", weights, extended[1], preferred_element_type=jnp.float32
    ).astype(jnp.bfloat16)
    attended = attended.reshape(-1, head_cols)[1 : 1 + tokens]
    term = jnp.dot(attended, w_out, preferred_element_type=jnp.float32).astype(jnp.bfloat16)
    return lax.optimization_barrier(term)


MESH = pl.DeviceIdType.MESH
LAG = 3
TAIL = 16
AHEAD = 2


def relay_kernel(
    x_hbm, wq_hbm, wo_hbm, kv_hbm, first_hbm, second_hbm,
    x_v, wq_v, wo_v, kv_v, x2_v, y_v, y2_v, acc_v, q_v, hq_v, ha_v, la_v, lb_v, att_v, r_v,
    x_sem, wq_sem, wo_sem, kv_sem, hq_send, hq_recv, ha_send, ha_recv,
    rel_send, rel_recv, out_sem,
):
    _, nq, _, cw = q_v.shape
    nf, fw = nq, x_v.shape[1] // nq
    halves, width, wide_cols = wq_v.shape
    quarters, cols, wide_features = wo_v.shape
    per_half, per_quarter = nq // halves, nf // quarters
    keys = kv_v.shape[2]
    half = keys // 2
    k, s = lax.axis_index("seq"), lax.axis_index("segment")
    nk, ns = lax.axis_size("seq"), lax.axis_size("segment")
    has_prev, has_next = k > 0, k < nk - 1
    has_in, has_out = s > 0, s < ns - 1
    prev = (lax.rem(k + nk - 1, nk), s)
    following = (lax.rem(k + 1, nk), s)
    below = (k, lax.rem(s + ns - 1, ns))
    above = (k, lax.rem(s + 1, ns))
    top, low = pl.ds(0, CH), pl.ds(CH, CH)
    last_row = lax.broadcasted_iota(jnp.int32, (CH, cw), 0) == CH - 1

    def head_cols(n):
        return pl.ds(pl.multiple_of(n * cw, cw), cw)

    def feature_cols(c):
        return pl.ds(pl.multiple_of(c * fw, fw), fw)

    def load_wq(h):
        source = wq_hbm.at[:, pl.ds(h * wide_cols, wide_cols)]
        return pltpu.make_async_copy(source, wq_v.at[h], wq_sem.at[h])

    def load_kv(t):
        return pltpu.make_async_copy(kv_hbm.at[t], kv_v.at[t], kv_sem.at[t])

    def load_wo(g):
        source = wo_hbm.at[:, pl.ds(g * wide_features, wide_features)]
        return pltpu.make_async_copy(source, wo_v.at[g], wo_sem.at[g])

    weights = [load_wq(h) for h in range(halves)] + [load_wo(g) for g in range(quarters)]

    def await_wq(h):
        load_wq(h).wait()
        weights[h + AHEAD].start()

    def halo_q(t, n):
        return pltpu.make_async_remote_copy(
            src_ref=q_v.at[t, n, top], dst_ref=hq_v.at[t, n],
            send_sem=hq_send, recv_sem=hq_recv.at[t, n],
            device_id=prev, device_id_type=MESH,
        )

    def halo_a(t, n):
        return pltpu.make_async_remote_copy(
            src_ref=ha_v.at[t, n], dst_ref=att_v.at[t, top, head_cols(n)],
            send_sem=ha_send, recv_sem=ha_recv.at[t, n],
            device_id=following, device_id_type=MESH,
        )

    parts = (pl.ds(0, CH), pl.ds(2 * CH - TAIL, TAIL), pl.ds(CH, CH - TAIL))

    def relay(b, g):
        rows, at = parts[b], pl.ds(pl.multiple_of(g * wide_features, wide_features), wide_features)
        return pltpu.make_async_remote_copy(
            src_ref=y_v.at[rows, at], dst_ref=x2_v.at[rows, at],
            send_sem=rel_send, recv_sem=rel_recv.at[b, g],
            device_id=above, device_id_type=MESH,
        )

    def store(t, g):
        buffer, target = ((y_v, first_hbm), (y2_v, second_hbm))[t]
        at = pl.ds(pl.multiple_of(g * wide_features, wide_features), wide_features)
        return pltpu.make_async_copy(buffer.at[:, at], target.at[:, at], out_sem.at[t])

    ones = jnp.ones((half, HD), jnp.bfloat16)

    def attend(block, t, n, span):
        at_keys = pl.ds(span * half, half)
        heads = []
        for h in range(cw // HD):
            at = pl.ds(pl.multiple_of(n * cw + h * HD, HD), HD)
            scores = lax.dot_general(
                block[:, h * HD:(h + 1) * HD], kv_v[t, 0, at_keys, at], (((1,), (1,)), ((), ())),
                preferred_element_type=jnp.float32,
            )
            most = jnp.max(scores, axis=1, keepdims=True)
            exponent = jnp.exp((scores - most) * HD ** (-0.5)).astype(jnp.bfloat16)
            values = jnp.concatenate([kv_v[t, 1, at_keys, at], ones], axis=1)
            both = jnp.dot(exponent, values, preferred_element_type=jnp.float32)
            heads.append(both[:, :HD] / both[:, HD:])
        return jnp.concatenate(heads, axis=1).astype(jnp.bfloat16)

    def loop(start, stop, body):
        def step(i, carry):
            body(i)
            return carry

        lax.fori_loop(start, stop, step, 0)

    def row_scale(ref, rows):
        def add(c, squares):
            block = ref[rows, feature_cols(c)].astype(jnp.float32)
            return squares + jnp.sum(block * block, axis=1, keepdims=True)

        squares = lax.fori_loop(0, nf, add, jnp.zeros((rows.size, 1), jnp.float32))
        return lax.rsqrt(squares / width + EPS)

    load_x = pltpu.make_async_copy(x_hbm, x_v, x_sem)
    load_x.start()
    weights[0].start()
    load_kv(0).start()
    for i in range(1, AHEAD):
        weights[i].start()

    barrier = pltpu.get_barrier_semaphore()
    pairs = ((has_prev, prev), (has_next, following), (has_in, below), (has_out, above))
    for exists, device in pairs:

        @pl.when(exists)
        def _(device=device):
            pl.semaphore_signal(barrier, inc=1, device_id=device, device_id_type=MESH)

    @pl.when(jnp.logical_not(has_next))
    def _():
        def clear(n):
            for t in range(TICKS):
                hq_v[t, n] = jnp.zeros_like(hq_v[t, n])

        loop(0, nq, clear)

    @pl.when(jnp.logical_not(has_prev))
    def _():
        def clear(n):
            for t in range(TICKS):
                att_v[t, top, head_cols(n)] = jnp.zeros((CH, cw), jnp.bfloat16)

        loop(0, nq, clear)

    @pl.when(jnp.logical_not(has_in))
    def _():
        def clear(c):
            x2_v[:, feature_cols(c)] = jnp.zeros((2 * CH, fw), jnp.bfloat16)

        loop(0, nf, clear)

    def clear_acc(h):
        acc_v[h] = jnp.zeros_like(acc_v[h])

    loop(0, halves, clear_acc)
    hq_v[0, nq] = jnp.zeros_like(hq_v[0, nq])
    load_x.wait()
    r_v[...] = jnp.broadcast_to(row_scale(x_v, pl.ds(0, 2 * CH)), r_v.shape)
    pl.semaphore_wait(barrier, sum(exists.astype(jnp.int32) for exists, _ in pairs))

    def keep_own(t, n, out):
        at = head_cols(n)
        att_v[t, low, at] = out
        la_v[:, at] = out[CH - TAIL:]

    def join(t):
        @pl.when(has_prev)
        def _():
            loop(0, nq, lambda n: halo_a(t, n).wait_recv())

        end = lax.broadcasted_iota(jnp.int32, la_v.shape, 0) == TAIL - 1
        top_end, low_end = pl.ds(CH - TAIL, TAIL), pl.ds(2 * CH - TAIL, TAIL)
        att_v[t, top_end] = jnp.where(end, la_v[...], att_v[t, top_end])
        att_v[t, low_end] = jnp.where(end, lb_v[...], att_v[t, low_end])

    def step(c, with_q, with_attention):
        other = c - LAG
        ready = other >= 0
        own, n = jnp.minimum(c - 1, nq - 1), jnp.maximum(other, 0)
        slot = jnp.where(ready, other, nq)
        if with_q:
            for h in range(1, halves):

                @pl.when(c == h * per_half)
                def _():
                    await_wq(h)

        if with_attention:

            @pl.when(jnp.logical_and(ready, has_next))
            def _():
                halo_q(0, n).wait_recv()

            own_block = jnp.where(last_row, q_v[0, own, top], q_v[0, own, low])
            halo_block = jnp.where(last_row, q_v[0, n, low], hq_v[0, slot])
        if with_q:
            at = pl.ds(pl.multiple_of(c % per_half * cw, cw), cw)
            weight = wq_v[c // per_half, :, at]
            total = jnp.dot(x_v[...], weight, preferred_element_type=jnp.float32)
            made = (total * r_v[:, :1]).astype(jnp.bfloat16)
        if with_attention:
            own_out = attend(own_block, 0, own, 0)
            halo_out = attend(halo_block, 0, n, 1)
        if with_q:
            q_v[0, c] = made

            @pl.when(has_prev)
            def _():
                halo_q(0, c).start()

        if with_attention:
            ha_v[0, slot] = halo_out
            lb_v[:, head_cols(n)] = halo_out[CH - TAIL:]

            @pl.when(jnp.logical_and(ready, has_next))
            def _():
                halo_a(0, n).start()

            keep_own(0, own, own_out)

    await_wq(0)
    step(0, True, False)
    load_kv(0).wait()
    loop(1, nq, lambda c: step(c, True, True))
    for copy in weights[halves + AHEAD:]:
        copy.start()
    load_kv(1).start()
    loop(nq, nq + LAG, lambda c: step(c, False, True))
    join(0)

    def project(t, c):
        at = pl.ds(pl.multiple_of(c % per_quarter * fw, fw), fw)
        weight = wo_v[c // per_quarter, :, at]
        term = jnp.dot(att_v[t], weight, preferred_element_type=jnp.float32)
        return term.astype(jnp.bfloat16).astype(jnp.float32)

    def first_chunk(c):
        g, at = c // per_quarter, feature_cols(c)

        @pl.when(c % per_quarter == 0)
        def _():
            load_wo(g).wait()

        residual = x_v[:, at].astype(jnp.float32)
        y_v[:, at] = (residual + project(0, c)).astype(jnp.bfloat16)

        @pl.when(c % per_quarter == per_quarter - 1)
        def _():
            @pl.when(has_out)
            def _():
                relay(0, g).start()
                relay(1, g).start()

            store(0, g).start()

    loop(0, nf, first_chunk)

    @pl.when(has_out)
    def _():
        loop(0, quarters, lambda g: relay(2, g).start())

    def await_relay(c, which):
        @pl.when(jnp.logical_and(c % per_quarter == 0, has_in))
        def _():
            for b in which:
                relay(b, c // per_quarter).wait_recv()

    def gather_early(c):
        await_relay(c, (0, 1))
        at = feature_cols(c)
        block = jnp.concatenate([x2_v[parts[0], at], x2_v[parts[1], at]], axis=0)
        for h in range(halves):
            made = jnp.dot(block, wq_v[h, at, :], preferred_element_type=jnp.float32)
            acc_v[h, parts[0]] += made[:CH]
            acc_v[h, parts[1]] += made[CH:]

    loop(0, nf, gather_early)

    def make_queries(rows):
        scale = row_scale(x2_v, rows)

        def query(n):
            at = pl.ds(pl.multiple_of(n % per_half * cw, cw), cw)
            q_v[1, n, rows] = (acc_v[n // per_half, rows, at] * scale).astype(jnp.bfloat16)

        loop(0, nq, query)

    for rows in parts[:2]:
        make_queries(rows)

    @pl.when(has_prev)
    def _():
        loop(0, nq, lambda n: halo_q(1, n).start())

    def gather_late(c):
        await_relay(c, (2,))
        at = feature_cols(c)
        block = x2_v[parts[2], at]
        for h in range(halves):
            acc_v[h, parts[2]] += jnp.dot(
                block, wq_v[h, at, :], preferred_element_type=jnp.float32
            )

    loop(0, nf, gather_late)
    make_queries(parts[2])
    load_kv(1).wait()

    def finish(n):
        @pl.when(has_next)
        def _():
            halo_q(1, n).wait_recv()

        block = q_v[1, n, low]
        halo_block = jnp.where(last_row, block, hq_v[1, n])
        own_block = jnp.where(last_row, q_v[1, n, top], block)
        halo_out = attend(halo_block, 1, n, 1)
        own_out = attend(own_block, 1, n, 0)
        ha_v[1, n] = halo_out
        lb_v[:, head_cols(n)] = halo_out[CH - TAIL:]

        @pl.when(has_next)
        def _():
            halo_a(1, n).start()

        keep_own(1, n, own_out)

    loop(0, nq, finish)
    join(1)

    def second_chunk(c):
        at = feature_cols(c)
        y2_v[:, at] = (x2_v[:, at].astype(jnp.float32) + project(1, c)).astype(jnp.bfloat16)

        @pl.when(c % per_quarter == per_quarter - 1)
        def _():
            store(1, c // per_quarter).start()

    loop(0, nf, second_chunk)

    halo = ha_v.at[:, pl.ds(0, nq)]

    @pl.when(has_prev)
    def _():
        pltpu.make_async_remote_copy(
            src_ref=halo, dst_ref=halo, send_sem=hq_send, recv_sem=hq_send,
            device_id=prev, device_id_type=MESH,
        ).wait_send()

    @pl.when(has_next)
    def _():
        pltpu.make_async_remote_copy(
            src_ref=halo, dst_ref=halo, send_sem=ha_send, recv_sem=ha_send,
            device_id=following, device_id_type=MESH,
        ).wait_send()

    @pl.when(has_out)
    def _():
        pltpu.make_async_remote_copy(
            src_ref=y_v, dst_ref=x2_v, send_sem=rel_send, recv_sem=rel_send,
            device_id=above, device_id_type=MESH,
        ).wait_send()

    pltpu.make_async_copy(y_v, first_hbm, out_sem.at[0]).wait()
    pltpu.make_async_copy(y2_v, second_hbm, out_sem.at[1]).wait()


def relay_call(stream, w_query, w_out, neighbour_kv):
    rows, width = stream.shape
    cols = w_query.shape[1]
    keys = neighbour_kv.shape[2]
    cw = 2 * HD
    nq = cols // cw
    bf16, dma = jnp.bfloat16, pltpu.SemaphoreType.DMA
    hbm = pl.BlockSpec(memory_space=pl.ANY)
    flops = TICKS * 2 * rows * cols * (2 * width + 4 * keys)
    read = 2 * (stream.size + w_query.size + w_out.size + neighbour_kv.size + 2 * stream.size)
    return pl.pallas_call(
        relay_kernel,
        out_shape=[jax.ShapeDtypeStruct(stream.shape, bf16)] * 2,
        in_specs=[hbm] * 4,
        out_specs=[hbm] * 2,
        scratch_shapes=[
            pltpu.VMEM((rows, width), bf16),
            pltpu.VMEM((4, width, cols // 4), bf16),
            pltpu.VMEM((4, cols, width // 4), bf16),
            pltpu.VMEM((TICKS, 2, keys, cols), bf16),
            pltpu.VMEM((rows, width), bf16),
            pltpu.VMEM((rows, width), bf16),
            pltpu.VMEM((rows, width), bf16),
            pltpu.VMEM((4, rows, cols // 4), jnp.float32),
            pltpu.VMEM((TICKS, nq, rows, cw), bf16),
            pltpu.VMEM((TICKS, nq + 1, CH, cw), bf16),
            pltpu.VMEM((TICKS, nq + 1, CH, cw), bf16),
            pltpu.VMEM((TAIL, cols), bf16),
            pltpu.VMEM((TAIL, cols), bf16),
            pltpu.VMEM((TICKS, rows, cols), bf16),
            pltpu.VMEM((rows, 128), jnp.float32),
            dma,
            dma((4,)),
            dma((4,)),
            dma((TICKS,)),
            dma,
            dma((TICKS, nq)),
            dma,
            dma((TICKS, nq)),
            dma,
            dma((3, 4)),
            dma((TICKS,)),
        ],
        compiler_params=pltpu.CompilerParams(
            collective_id=0, has_side_effects=True, vmem_limit_bytes=60 * 2**20
        ),
        cost_estimate=pl.CostEstimate(flops=flops, bytes_accessed=read, transcendentals=0),
    )(stream, w_query, w_out, neighbour_kv)


def copy_kernel(first_in, second_in, first_out, second_out, held, in_sem, out_sem):
    moves = []
    for i, (source, target) in enumerate(((first_in, first_out), (second_in, second_out))):
        rows = source.shape[0] // in_sem.shape[1]
        for j in range(in_sem.shape[1]):
            at = pl.ds(j * rows, rows)
            fetch = pltpu.make_async_copy(source.at[at], held.at[i, at], in_sem.at[i, j])
            store = pltpu.make_async_copy(held.at[i, at], target.at[at], out_sem.at[i, j])
            fetch.start()
            moves.append((fetch, store))
    for fetch, store in moves:
        fetch.wait()
        store.start()
    for fetch, store in moves:
        store.wait()


def copied(first, second):
    hbm = pl.BlockSpec(memory_space=pl.ANY)
    return pl.pallas_call(
        copy_kernel,
        out_shape=[jax.ShapeDtypeStruct(a.shape, a.dtype) for a in (first, second)],
        in_specs=[hbm] * 2,
        out_specs=[hbm] * 2,
        scratch_shapes=[
            pltpu.VMEM((2,) + first.shape, first.dtype),
            pltpu.SemaphoreType.DMA((2, 4)),
            pltpu.SemaphoreType.DMA((2, 4)),
        ],
        compiler_params=pltpu.CompilerParams(vmem_limit_bytes=60 * 2**20),
        cost_estimate=pl.CostEstimate(flops=0, bytes_accessed=8 * first.size, transcendentals=0),
    )(first, second)


def fits(stream, w_query, neighbour_kv):
    rows, width = stream.shape
    cols = w_query.shape[1]
    return (
        lax.axis_size("segment") == SECT
        and rows == 2 * CH
        and neighbour_kv.shape[2] == 2 * NEIGH * NBL
        and cols % (8 * HD) == 0
        and width % (cols // (2 * HD) * 128) == 0
        and cols // (2 * HD) == 8
        and 2 * width * cols * 2 + neighbour_kv.size * 2 <= 42 * 2**20
    )


def per_device(stream, w_query, w_out, neighbour_kv):
    if fits(stream, w_query, neighbour_kv):
        return tuple(copied(*relay_call(stream, w_query, w_out, neighbour_kv)))
    groups_per = lax.axis_size("segment") // SECT
    head_group = lax.axis_index("segment") % groups_per
    total_bits = groups_per.bit_length() - 1
    bit_order = list(range(total_bits))
    edge_rows = NEIGH * NBL
    edges = passed_along(neighbour_kv[:, :, neighbour_kv.shape[2] - edge_rows :, :], "seq", 1)
    current = stream
    whole = assemble(current, head_group, bit_order, total_bits)
    outputs = []
    for tick_no in range(TICKS):
        term = local_layer(whole, neighbour_kv[tick_no], edges[tick_no], w_query, w_out)
        summed = share_sums(term, head_group, bit_order, total_bits)
        result = (current.astype(jnp.float32) + summed).astype(jnp.bfloat16)
        outputs.append(result)
        if tick_no + 1 < TICKS:
            current = passed_along(result, "segment", groups_per)
            whole = assemble(current, head_group, bit_order, total_bits)
    return (outputs[0], outputs[TICKS - 1])


def solution(mesh):
    placed = (
        P("seq", "segment"),
        P(None, "segment"),
        P("segment", None),
        P(None, None, "seq", "segment"),
    )
    return jax.shard_map(
        per_device,
        mesh=mesh,
        in_specs=placed,
        out_specs=(P("seq", "segment"), P("seq", "segment")),
        check_vma=False,
    )
```
